128 devices in a mesh: dp: 16 (over y_hi, x, core), tensor: 8 (over y_lo, z).
Axes of the slice: x: 4, y: 4 (y_hi: 2, y_lo: 2; y = y_hi * 2 + y_lo), z: 4, core: 2. Of those that a mesh axis runs over, the one named last changes fastest.
Arguments:
- hidden_in: bfloat16 [16384, 1024], P(('dp', 'tensor')), may hold values from -25 to 25
- cotangent: bfloat16 [16384, 1024], P(('dp', 'tensor')), may hold values from -6 to 6
- norm_gain: float32 [2, 2, 1024], replicated, may hold values from 0.5 to 1.5
- norm_shift: float32 [2, 2, 1024], replicated, may hold values from -4 to 4
- inward: bfloat16 [2, 1024, 3, 1024], P(None, None, None, 'tensor'), may hold values from -0.1875 to 0.1875
- inward_bias: float32 [2, 2, 1024], P(None, None, 'tensor'), may hold values from -4 to 4
- outward: bfloat16 [2, 1024, 1024], P(None, 'tensor'), may hold values from -0.75 to 0.75
- outward_bias: float32 [2, 1024], replicated, may hold values from -4 to 4
- expand: bfloat16 [2, 1024, 4096], P(None, None, 'tensor'), may hold values from -0.1875 to 0.1875
- expand_bias: float32 [2, 4096], P(None, 'tensor'), may hold values from -4 to 4
- shrink: bfloat16 [2, 4096, 1024], P(None, 'tensor'), may hold values from -0.125 to 0.125
- shrink_bias: float32 [2, 1024], replicated, may hold values from -4 to 4
Outputs:
- hidden_out: float32 [16384, 1024], P(('dp', 'tensor'))
- grad_hidden: float32 [16384, 1024], P(('dp', 'tensor'))
- grad_gain: float32 [2, 2, 1024], replicated
- grad_shift: float32 [2, 2, 1024], replicated
- grad_inward: float32 [2, 1024, 3, 1024], P(None, 'dp', None, 'tensor')
- grad_inward_bias: float32 [2, 2, 1024], P(None, None, 'tensor')
- grad_outward: float32 [2, 1024, 1024], P(None, 'tensor', 'dp')
- grad_outward_bias: float32 [2, 1024], replicated
- grad_expand: float32 [2, 1024, 4096], P(None, 'dp', 'tensor')
- grad_expand_bias: float32 [2, 4096], P(None, 'tensor')
- grad_shrink: float32 [2, 4096, 1024], P(None, 'tensor', 'dp')
- grad_shrink_bias: float32 [2, 1024], replicated
The draws below stay inside these ranges and needn't reach their ends.
All inputs are finite; a program needn't handle non-finite values.
Results may differ from the reference program's by a relative error of at most 0.025.
Values may be sent and summed in bfloat16 or wider, within the bound.
No kernel may reach another device: no remote copies, remote signals or barrier semaphores. Data moves between devices by JAX's collectives and lax.ppermute only.
A program may use at most 128 MiB of HBM per device.

```python
import math
import jax
import jax.numpy as jnp
from jax import lax

D = 1024
HEADS = 16
HEAD_DIM = 64
FF = 4096
LAYERS = 2
SEQ_LEN = 1024
SEQS = 16
TOKENS = 16384


def draw_hidden_in(key, part):
    key = jax.random.fold_in(key, 5)
    row_key, column_key, sample_key = jax.random.split(key, 3)
    row_scale = jnp.exp(jax.random.uniform(row_key, (TOKENS, 1), jnp.float32, math.log(0.5), math.log(5.0)))
    column_scale = jnp.exp(jax.random.uniform(column_key, (1, D), jnp.float32, math.log(0.5), math.log(5.0)))
    samples = jnp.clip(jax.random.normal(sample_key, (TOKENS, D), jnp.float32), -4.0, 4.0)
    return (0.25 * samples * row_scale * column_scale).astype(jnp.bfloat16)


def draw_cotangent(key, part):
    key = jax.random.fold_in(key, 9)
    position = jnp.arange(TOKENS, dtype=jnp.float32)[:, None] / TOKENS
    samples = jnp.clip(jax.random.normal(key, (TOKENS, D), jnp.float32), -4.0, 4.0)
    ramp = 0.5 + position
    return (samples * ramp).astype(jnp.bfloat16)


def level_of(rng, shape, shards, low, largest):
    level, own = 1.0, jax.random.fold_in(rng, 6)
    for dim, shards_of in shards:
        steps = jnp.exp(jax.random.uniform(jax.random.fold_in(own, dim), (shards_of,), jnp.float32, low / len(shards), largest / len(shards)))
        level = level * jnp.repeat(steps, shape[dim] // shards_of).reshape([-1 if axis == dim else 1 for axis in range(len(shape))])
    return level


def scatter_about(own_key, extent, scale, bound, cuts=(), kind=jnp.bfloat16):
    array = jax.random.normal(own_key, extent, jnp.float32) * scale
    if len(cuts) > 0:
        array = level_of(own_key, extent, cuts, -0.22, 0.18) * array
    return jnp.clip(array, min=-bound, max=bound).astype(kind)


def setup_inputs(seed: int = 0) -> dict:
    seeds = jax.random.split(jax.random.key(seed), 13)
    return {
        "hidden_in": draw_hidden_in(jax.random.fold_in(seeds[12], 71), 0),
        "cotangent": draw_cotangent(jax.random.fold_in(seeds[12], 71), 0),
        "norm_gain": jnp.clip(1.0 + 0.1 * jax.random.normal(seeds[2], (LAYERS, 2, D), jnp.float32), 0.5, 1.5),
        "norm_shift": scatter_about(seeds[3], (LAYERS, 2, D), 0.3, 4.0, (), jnp.float32),
        "inward": scatter_about(seeds[4], (LAYERS, D, 3, D), D ** -0.5, 0.1875, ((3, 8),)),
        "inward_bias": scatter_about(seeds[5], (LAYERS, 2, D), 0.3, 4.0, ((2, 8),), jnp.float32),
        "outward": scatter_about(seeds[6], (LAYERS, D, D), (D // 16) ** -0.5, 0.75, ((1, 8),)),
        "outward_bias": scatter_about(seeds[7], (LAYERS, D), 0.3, 4.0, (), jnp.float32),
        "expand": scatter_about(seeds[8], (LAYERS, D, FF), D ** -0.5, 0.1875, ((2, 8),)),
        "expand_bias": scatter_about(seeds[9], (LAYERS, FF), 0.3, 4.0, ((1, 8),), jnp.float32),
        "shrink": scatter_about(seeds[10], (LAYERS, FF, D), (FF // 2) ** -0.5, 0.125, ((1, 8),)),
        "shrink_bias": scatter_about(seeds[11], (LAYERS, D), 0.3, 4.0, (), jnp.float32),
    }


@jax.custom_vjp
def low(v):
    return lax.optimization_barrier(v.astype(jnp.bfloat16)).astype(jnp.float32)

@jax.custom_vjp
def low_back(v):
    return v

def low_keep(v):
    return (low(v), None)

def low_pass(kept, grad):
    return (grad,)

def back_keep(v):
    return (v, None)

def back_low(kept, grad):
    return (low(grad),)
low.defvjp(low_keep, low_pass)
low_back.defvjp(back_keep, back_low)
EPS_NORM = 1e-05
NEG_FILL = -1000000000.0
PRECISE = lax.Precision.HIGHEST

def layer_norm(stream, norm_gain, norm_shift):
    center = stream - lax.optimization_barrier(jnp.mean(stream, -1, keepdims=True))
    spread = lax.optimization_barrier(jnp.mean(center * center, -1, keepdims=True))
    return center * lax.rsqrt(spread + EPS_NORM) * norm_gain + norm_shift

def gelu_tanh(values):
    return 0.5 * values * (1.0 + jnp.tanh(0.7978845608028654 * (values + 0.044715 * values * values * values)))

def attend(pieces):
    queries, key_rows, value_rows = pieces
    scores = jnp.einsum('qhd,khd->hqk', queries, key_rows, precision=PRECISE) * HEAD_DIM ** (-0.5)
    scores = low_back(scores)
    place = jnp.arange(SEQ_LEN)
    causal = place[:, None] >= place[None, :]
    scores = jnp.where(causal[None], scores, NEG_FILL)
    row_peak = lax.optimization_barrier(jnp.max(scores, -1, keepdims=True))
    weights = jnp.exp(scores - row_peak)
    weights = weights / lax.optimization_barrier(jnp.sum(weights, -1, keepdims=True))
    return jnp.einsum('hqk,khd->qhd', low(weights), value_rows, precision=PRECISE)

def split_heads(flat):
    return flat.reshape(SEQS, SEQ_LEN, HEADS, HEAD_DIM)

def forward(hidden_in, norm_gain, norm_shift, inward, inward_bias, outward, outward_bias, expand, expand_bias, shrink, shrink_bias):
    stream = hidden_in
    for layer_index in range(LAYERS):
        normed = low(layer_norm(stream, norm_gain[layer_index, 0], norm_shift[layer_index, 0]))
        projected = jnp.einsum('td,dcf->tcf', normed, inward[layer_index], precision=PRECISE)
        queries = low_back(low(projected[:, 0] + inward_bias[layer_index, 0]))
        key_rows = low_back(low(projected[:, 1]))
        value_rows = low_back(low(projected[:, 2] + inward_bias[layer_index, 1]))
        attended = lax.map(jax.checkpoint(attend), (split_heads(queries), split_heads(key_rows), split_heads(value_rows)))
        attended = low_back(low(attended.reshape(TOKENS, D)))
        branch = low_back(jnp.dot(attended, outward[layer_index], precision=PRECISE) + outward_bias[layer_index])
        middle = stream + branch
        normed_mid = low(layer_norm(middle, norm_gain[layer_index, 1], norm_shift[layer_index, 1]))
        hidden_pre = low_back(jnp.dot(normed_mid, expand[layer_index], precision=PRECISE) + expand_bias[layer_index])
        activated = low(gelu_tanh(hidden_pre))
        branch_mlp = low_back(jnp.dot(activated, shrink[layer_index], precision=PRECISE) + shrink_bias[layer_index])
        stream = middle + branch_mlp
    return stream

def reference(hidden_in, cotangent, norm_gain, norm_shift, inward, inward_bias, outward, outward_bias, expand, expand_bias, shrink, shrink_bias):
    hidden_out, backward = jax.vjp(forward, hidden_in.astype(jnp.float32), norm_gain.astype(jnp.float32), norm_shift.astype(jnp.float32), inward.astype(jnp.float32), inward_bias.astype(jnp.float32), outward.astype(jnp.float32), outward_bias.astype(jnp.float32), expand.astype(jnp.float32), expand_bias.astype(jnp.float32), shrink.astype(jnp.float32), shrink_bias.astype(jnp.float32))
    grads = backward(cotangent.astype(jnp.float32))
    return (hidden_out, grads[0], grads[1], grads[2], grads[3], grads[4], grads[5], grads[6], grads[7], grads[8], grads[9], grads[10])
```

```python
import jax
import jax.numpy as jnp
from jax import lax
from jax.sharding import Mesh
from jax.sharding import PartitionSpec as P

HEAD_DIM = 64
LAYERS = 2
EPS_NORM = 1e-05
NEG_FILL = -1000000000.0
BF = jnp.bfloat16
F32 = jnp.float32
RINGS = {"z": ("z",), "x": ("x",), "y": ("yh", "yl")}


def layer_norm(stream, norm_gain, norm_shift):
    center = stream - jnp.mean(stream, -1, keepdims=True)
    spread = jnp.mean(center * center, -1, keepdims=True)
    return center * lax.rsqrt(spread + EPS_NORM) * norm_gain + norm_shift


def gelu_tanh(values):
    return (
        0.5
        * values
        * (1.0 + jnp.tanh(0.7978845608028654 * (values + 0.044715 * values * values * values)))
    )


def tokens_inner(left, right):
    return lax.dot_general(left, right, (((0,), (0,)), ((), ())), preferred_element_type=F32)


def against_rows(left, right):
    return lax.dot_general(left, right, (((1,), (1,)), ((), ())), preferred_element_type=F32)


def ring(values, axis, step):
    return lax.ppermute(values, RINGS[axis], [(i, (i + step) % 4) for i in range(4)])


def swap_cores(values):
    return lax.ppermute(values, "c", [(0, 1), (1, 0)])


def swap_halves(values):
    return lax.ppermute(values, ("c", "yl"), [(0, 0), (1, 2), (2, 1), (3, 3)])


def y_pairs(rule):
    pairs = []
    for y in range(4):
        for core in range(2):
            target = rule(y, core)
            if target is not None:
                y2, core2 = target[0] % 4, target[1]
                pairs.append(
                    ((y // 2) * 4 + core * 2 + y % 2, (y2 // 2) * 4 + core2 * 2 + y2 % 2)
                )
    return pairs


def fetch_weights(values, step):
    return lax.ppermute(
        values,
        ("yh", "c", "yl"),
        y_pairs(lambda y, c: (y - step, y % 2) if c == y % 2 else (y, y % 2)),
    )


def gather_rows(values):
    before = ring(values, "z", 1)
    after = ring(values, "z", -1)
    across = ring(values, "z", 2)
    mine = jnp.concatenate([values, before, after, across])
    return jnp.concatenate([mine, swap_cores(mine)])


def scatter_rows(partial):
    half = partial.shape[0] // 2
    rows = half // 4
    other = swap_cores(partial[half:].astype(BF))
    both = partial[:half] + other.astype(F32)
    low = both.astype(BF)
    from_after = ring(low[rows : 2 * rows], "z", -1)
    from_before = ring(low[2 * rows : 3 * rows], "z", 1)
    from_across = ring(low[3 * rows :], "z", 2)
    return (
        both[:rows]
        + from_after.astype(F32)
        + from_before.astype(F32)
        + from_across.astype(F32)
    )


def scatter_grads(grad):
    columns = grad.shape[1]
    blocks = grad.reshape(2, 4, 128, columns)
    place = lax.axis_index("x")

    def pick(step):
        return lax.dynamic_index_in_dim(blocks, (place + step) % 4, 1, keepdims=False)

    summed = (
        pick(0).astype(F32)
        + ring(pick(1).astype(BF), "x", 1).astype(F32)
        + ring(pick(3).astype(BF), "x", -1).astype(F32)
        + ring(pick(2).astype(BF), "x", 2).astype(F32)
    )
    high = lax.axis_index("yh")
    y = high * 2 + lax.axis_index("yl")

    def pick_high(index):
        return lax.dynamic_index_in_dim(summed, index, 0, keepdims=False)

    axes = ("yh", "c", "yl")
    up = lax.ppermute(
        pick_high(((y + 1) % 4) // 2).astype(BF),
        axes,
        y_pairs(lambda y, c: (y + 1, c) if c != y % 2 else None),
    )
    down = lax.ppermute(
        pick_high(((y + 3) % 4) // 2).astype(BF),
        axes,
        y_pairs(lambda y, c: (y + 3, c) if c != y % 2 else None),
    )
    far = lax.ppermute(
        pick_high(1 - high).astype(BF),
        axes,
        y_pairs(lambda y, c: (y + 2, c) if c == y % 2 else None),
    )
    total = pick_high(high) + up.astype(F32) + down.astype(F32) + far.astype(F32)
    core = lax.axis_index("c")
    halves = total.reshape(2, 64, columns)
    keep = lax.dynamic_index_in_dim(halves, core, 0, keepdims=False)
    give = lax.dynamic_index_in_dim(halves, 1 - core, 0, keepdims=False)
    got = lax.ppermute(give, ("c", "yl"), [(0, 2), (3, 1)])
    return jnp.where(core == lax.axis_index("yl"), keep, got)


def sum_everywhere(values):
    values = values + swap_cores(values)
    for axis in ("z", "x", "y"):
        values = (values + ring(values, axis, 2)) + (
            ring(values, axis, 1) + ring(values, axis, -1)
        )
    return values


def split_heads(flat):
    return flat.reshape(flat.shape[0], flat.shape[1] // HEAD_DIM, HEAD_DIM)


def row_places():
    core, z = lax.axis_index("c"), lax.axis_index("z")
    blocks = jnp.stack([cc * 4 + (z + dz) % 4 for cc in (core, 1 - core) for dz in (0, 3, 1, 2)])
    return (blocks[:, None] * 128 + lax.iota(jnp.int32, 128)[None, :]).reshape(-1)


def masked_scores(queries, keys, mask):
    scores = jnp.einsum("qhd,khd->hqk", queries, keys, preferred_element_type=F32)
    return jnp.where(mask, scores * HEAD_DIM ** (-0.5), NEG_FILL)


def attend_forward(queries, keys, values, mask):
    scores = masked_scores(split_heads(queries), split_heads(keys), mask)
    peak = jnp.max(scores, -1, keepdims=True)
    weights = jnp.exp(scores - peak)
    total = jnp.sum(weights, -1, keepdims=True)
    weights = weights / total
    mixed = jnp.einsum(
        "hqk,khd->qhd", weights.astype(BF), split_heads(values), preferred_element_type=F32
    )
    return mixed.astype(BF).reshape(queries.shape), peak + jnp.log(total)


def attend_backward(queries, keys, values, grad_out, log_totals, mask):
    q, k, v, do = (split_heads(m) for m in (queries, keys, values, grad_out))
    scale = HEAD_DIM ** (-0.5)
    weights = jnp.exp(masked_scores(q, k, mask) - log_totals)
    grad_weights = jnp.einsum("qhd,khd->hqk", do, v, preferred_element_type=F32)
    grad_scores = (
        weights * (grad_weights - jnp.sum(weights * grad_weights, -1, keepdims=True))
    ).astype(BF)
    dq = jnp.einsum("hqk,khd->qhd", grad_scores, k, preferred_element_type=F32) * scale
    dk = jnp.einsum("hqk,qhd->khd", grad_scores, q, preferred_element_type=F32) * scale
    dv = jnp.einsum("hqk,qhd->khd", weights.astype(BF), do, preferred_element_type=F32)
    return tuple(m.astype(BF).reshape(queries.shape) for m in (dq, dk, dv))


def per_device(
    hidden_in,
    cotangent,
    norm_gain,
    norm_shift,
    inward,
    inward_bias,
    outward,
    outward_bias,
    expand,
    expand_bias,
    shrink,
    shrink_bias,
):
    stream = swap_halves(hidden_in).astype(F32)
    columns = inward.shape[3]
    w_in, w_out, w_up, w_down = [], [], [], []
    for layer in range(LAYERS):
        w_in.append(fetch_weights(inward[layer].reshape(-1, 3 * columns), 1))
        if layer == 0:
            biases = fetch_weights(
                jnp.concatenate([inward_bias.reshape(-1, 128), expand_bias.reshape(-1, 128)]), -1
            )
            bias_in = biases[:4].reshape(LAYERS, 2, columns)
            bias_up = biases[4:].reshape(LAYERS, -1)
        w_out.append(fetch_weights(outward[layer], -1))
        w_up.append(fetch_weights(expand[layer], -1))
        w_down.append(fetch_weights(shrink[layer], 1))
    cotangent = swap_halves(cotangent)

    places = row_places()
    mask = (places[:, None] >= places[None, :])[None]
    saved = []
    for layer in range(LAYERS):
        normed = layer_norm(stream, norm_gain[layer, 0], norm_shift[layer, 0]).astype(BF)
        normed_all = gather_rows(normed)
        projected = jnp.dot(normed_all, w_in[layer], preferred_element_type=F32)
        queries = (projected[:, :columns] + bias_in[layer, 0]).astype(BF)
        keys = projected[:, columns : 2 * columns].astype(BF)
        values = (projected[:, 2 * columns :] + bias_in[layer, 1]).astype(BF)
        attended, log_totals = attend_forward(queries, keys, values, mask)
        middle = stream + (
            scatter_rows(jnp.dot(attended, w_out[layer], preferred_element_type=F32))
            + outward_bias[layer]
        )
        normed_mid = layer_norm(middle, norm_gain[layer, 1], norm_shift[layer, 1]).astype(BF)
        mid_all = gather_rows(normed_mid)
        hidden_pre = (
            jnp.dot(mid_all, w_up[layer], preferred_element_type=F32) + bias_up[layer]
        )
        activated = gelu_tanh(hidden_pre).astype(BF)
        result = middle + (
            scatter_rows(jnp.dot(activated, w_down[layer], preferred_element_type=F32))
            + shrink_bias[layer]
        )
        saved.append(
            (stream, normed_all, queries, keys, values, attended, log_totals, middle, mid_all,
             hidden_pre, activated)
        )
        stream = result
    hidden_out = swap_halves(stream)

    grad_stream = cotangent.astype(F32)
    gains, shifts, sums_out, sums_down, sums_in, sums_up = {}, {}, {}, {}, {}, {}
    grads_mlp, grads_attn = [None] * LAYERS, [None] * LAYERS
    for layer in reversed(range(LAYERS)):
        (stream, normed_all, queries, keys, values, attended, log_totals, middle, mid_all,
         hidden_pre, activated) = saved[layer]
        dy = grad_stream.astype(BF)
        sums_down[layer] = jnp.sum(dy, 0, dtype=F32)
        dy_all = gather_rows(dy)
        grad_act = against_rows(dy_all, w_down[layer])
        du = jax.vjp(gelu_tanh, hidden_pre)[1](grad_act)[0].astype(BF)
        sums_up[layer] = jnp.sum(du, 0, dtype=F32)
        dh = scatter_rows(against_rows(du, w_up[layer]))
        grads_mlp[layer] = scatter_grads(
            jnp.concatenate(
                [tokens_inner(dy_all, activated), tokens_inner(mid_all, du)], 1
            )
        )
        back_mid = jax.vjp(layer_norm, middle, norm_gain[layer, 1], norm_shift[layer, 1])[1]
        grad_part, gains[layer, 1], shifts[layer, 1] = back_mid(dh)
        grad_middle = grad_stream + grad_part
        dz = grad_middle.astype(BF)
        sums_out[layer] = jnp.sum(dz, 0, dtype=F32)
        dz_all = gather_rows(dz)
        do = against_rows(dz_all, w_out[layer]).astype(BF)
        dq, dk, dv = attend_backward(queries, keys, values, do, log_totals, mask)
        sums_in[layer] = jnp.stack([jnp.sum(dq, 0, dtype=F32), jnp.sum(dv, 0, dtype=F32)])
        dqkv = jnp.concatenate([dq, dk, dv], 1)
        da = scatter_rows(against_rows(dqkv, w_in[layer]))
        grads_attn[layer] = scatter_grads(
            jnp.concatenate(
                [tokens_inner(dz_all, attended), tokens_inner(normed_all, dqkv)], 1
            )
        )
        back_in = jax.vjp(layer_norm, stream, norm_gain[layer, 0], norm_shift[layer, 0])[1]
        grad_first, gains[layer, 0], shifts[layer, 0] = back_in(da)
        grad_stream = grad_middle + grad_first
    grad_hidden = swap_halves(grad_stream)

    shard = lax.axis_index("c") * 4 + lax.axis_index("z")
    own = lax.axis_index("yl") * 4 + lax.axis_index("z")
    both = range(LAYERS)
    up = jnp.stack([sums_up[n] for n in both])[:, None]
    qv = jnp.stack([sums_in[n] for n in both])[:, :, None]
    up = lax.dynamic_update_slice_in_dim(jnp.zeros((LAYERS, 8, up.shape[2]), F32), up, shard, 1)
    qv = lax.dynamic_update_slice_in_dim(jnp.zeros((LAYERS, 2, 8, columns), F32), qv, shard, 2)
    vectors = jnp.concatenate(
        [
            m.reshape(-1, 128)
            for m in (
                [gains[n, i] for n in both for i in (0, 1)]
                + [shifts[n, i] for n in both for i in (0, 1)]
                + [sums_out[n] for n in both]
                + [sums_down[n] for n in both]
                + [up, qv]
            )
        ]
    )
    vectors = sum_everywhere(vectors)
    grad_gain = vectors[:32].reshape(LAYERS, 2, 1024)
    grad_shift = vectors[32:64].reshape(LAYERS, 2, 1024)
    grad_out_bias = vectors[64:80].reshape(LAYERS, 1024)
    grad_down_bias = vectors[80:96].reshape(LAYERS, 1024)
    up = vectors[96:160].reshape(LAYERS, 8, -1)
    qv = vectors[160:].reshape(LAYERS, 2, 8, columns)
    grad_up_bias = lax.dynamic_index_in_dim(up, own, 1, keepdims=False)
    grad_in_bias = lax.dynamic_index_in_dim(qv, own, 2, keepdims=False)

    width = activated.shape[1]
    return (
        hidden_out,
        grad_hidden,
        grad_gain,
        grad_shift,
        jnp.stack([g[:, columns:].reshape(-1, 3, columns) for g in grads_attn]),
        grad_in_bias,
        jnp.stack([g[:, :columns].T for g in grads_attn]),
        grad_out_bias,
        jnp.stack([g[:, width:] for g in grads_mlp]),
        grad_up_bias,
        jnp.stack([g[:, :width].T for g in grads_mlp]),
        grad_down_bias,
    )


def solution(mesh):
    fine = Mesh(mesh.devices.reshape(2, 4, 2, 2, 4), ("yh", "x", "c", "yl", "z"))
    dp, tensor = ("yh", "x", "c"), ("yl", "z")
    rows = P(dp + tensor, None)
    return jax.shard_map(
        per_device,
        mesh=fine,
        in_specs=(
            rows,
            rows,
            P(),
            P(),
            P(None, None, None, tensor),
            P(None, None, tensor),
            P(None, tensor, None),
            P(),
            P(None, None, tensor),
            P(None, tensor),
            P(None, tensor, None),
            P(),
        ),
        out_specs=(
            rows,
            rows,
            P(),
            P(),
            P(None, dp, None, tensor),
            P(None, None, tensor),
            P(None, tensor, dp),
            P(),
            P(None, dp, tensor),
            P(None, tensor),
            P(None, tensor, dp),
            P(),
        ),
        check_vma=False,
    )
```

```python
import jax
import jax.numpy as jnp
from jax import lax
from jax.sharding import Mesh
from jax.sharding import PartitionSpec as P

HEAD_DIM = 64
LAYERS = 2
EPS_NORM = 1e-05
NEG_FILL = -1000000000.0
BF = jnp.bfloat16
F32 = jnp.float32
RINGS = {"z": ("z",), "x": ("x",), "y": ("yh", "yl")}


def layer_norm(stream, norm_gain, norm_shift):
    center = stream - jnp.mean(stream, -1, keepdims=True)
    spread = jnp.mean(center * center, -1, keepdims=True)
    return center * lax.rsqrt(spread + EPS_NORM) * norm_gain + norm_shift


def gelu_tanh(values):
    return (
        0.5
        * values
        * (1.0 + jnp.tanh(0.7978845608028654 * (values + 0.044715 * values * values * values)))
    )


def tokens_inner(left, right):
    return lax.dot_general(left, right, (((0,), (0,)), ((), ())), preferred_element_type=F32)


def against_rows(left, right):
    return lax.dot_general(left, right, (((1,), (1,)), ((), ())), preferred_element_type=F32)


def ring(values, axis, step):
    return lax.ppermute(values, RINGS[axis], [(i, (i + step) % 4) for i in range(4)])


def swap_cores(values):
    return lax.ppermute(values, "c", [(0, 1), (1, 0)])


def swap_halves(values):
    return lax.ppermute(values, ("c", "yl"), [(0, 0), (1, 2), (2, 1), (3, 3)])


def y_pairs(rule):
    pairs = []
    for y in range(4):
        for core in range(2):
            target = rule(y, core)
            if target is not None:
                y2, core2 = target[0] % 4, target[1]
                pairs.append(
                    ((y // 2) * 4 + core * 2 + y % 2, (y2 // 2) * 4 + core2 * 2 + y2 % 2)
                )
    return pairs


def fetch_weights(values, step):
    return lax.ppermute(
        values,
        ("yh", "c", "yl"),
        y_pairs(lambda y, c: (y - step, y % 2) if c == y % 2 else (y, y % 2)),
    )


def gather_rows(values):
    before = ring(values, "z", 1)
    after = ring(values, "z", -1)
    across = ring(values, "z", 2)
    mine = jnp.concatenate([values, before, after, across])
    return jnp.concatenate([mine, swap_cores(mine)])


def scatter_rows(partial):
    half = partial.shape[0] // 2
    rows = half // 4
    other = swap_cores(partial[half:].astype(BF))
    both = partial[:half] + other.astype(F32)
    low = both.astype(BF)
    from_after = ring(low[rows : 2 * rows], "z", -1)
    from_before = ring(low[2 * rows : 3 * rows], "z", 1)
    from_across = ring(low[3 * rows :], "z", 2)
    total = (
        both[:rows]
        + from_after.astype(F32)
        + from_before.astype(F32)
        + from_across.astype(F32)
    )
    return total, low


def scatter_grads(grads):
    count, _, columns = grads.shape
    blocks = grads.reshape(count, 2, 4, 128, columns)
    place = lax.axis_index("x")

    def pick(step):
        return lax.dynamic_index_in_dim(blocks, (place + step) % 4, 2, keepdims=False)

    summed = (
        pick(0).astype(F32)
        + ring(pick(1), "x", 1).astype(F32)
        + ring(pick(3), "x", -1).astype(F32)
        + ring(pick(2), "x", 2).astype(F32)
    )
    high, low_place, core = lax.axis_index("yh"), lax.axis_index("yl"), lax.axis_index("c")

    def pick_high(index):
        return jnp.where(index == 0, summed[:, 0], summed[:, 1])

    axes = ("yh", "c", "yl")
    y = high * 2 + low_place
    up = lax.ppermute(
        pick_high(((y + 1) % 4) // 2).astype(BF),
        axes,
        y_pairs(lambda y, c: (y + 1, c) if c != y % 2 else None),
    )
    down = lax.ppermute(
        pick_high(((y + 3) % 4) // 2).astype(BF),
        axes,
        y_pairs(lambda y, c: (y + 3, c) if c != y % 2 else None),
    )
    far = lax.ppermute(
        pick_high(1 - high).astype(BF),
        axes,
        y_pairs(lambda y, c: (y + 2, c) if c == y % 2 else None),
    )
    total = pick_high(high) + up.astype(F32) + down.astype(F32) + far.astype(F32)
    first, second = total[:, :64], total[:, 64:]
    keep = jnp.where(core == 0, first, second)
    give = jnp.where(core == 0, second, first)
    got = lax.ppermute(give, ("c", "yl"), [(0, 2), (3, 1)])
    return jnp.where(core == low_place, keep, got)


def sum_everywhere(values):
    values = values + swap_cores(values)
    for axis in ("z", "x", "y"):
        values = (values + ring(values, axis, 2)) + (
            ring(values, axis, 1) + ring(values, axis, -1)
        )
    return values


def split_heads(flat):
    return flat.reshape(flat.shape[0], flat.shape[1] // HEAD_DIM, HEAD_DIM)


def row_places():
    core, z = lax.axis_index("c"), lax.axis_index("z")
    blocks = jnp.stack([cc * 4 + (z + dz) % 4 for cc in (core, 1 - core) for dz in (0, 3, 1, 2)])
    return (blocks[:, None] * 128 + lax.iota(jnp.int32, 128)[None, :]).reshape(-1)


def masked_scores(queries, keys, mask):
    scores = jnp.einsum("qhd,khd->hqk", queries, keys, preferred_element_type=F32)
    return jnp.where(mask, scores * HEAD_DIM ** (-0.5), NEG_FILL)


def attend_forward(queries, keys, values, mask):
    scores = masked_scores(split_heads(queries), split_heads(keys), mask)
    peak = jnp.max(scores, -1, keepdims=True)
    weights = jnp.exp(scores - peak)
    total = jnp.sum(weights, -1, keepdims=True)
    weights = weights / total
    mixed = jnp.einsum(
        "hqk,khd->qhd", weights.astype(BF), split_heads(values), preferred_element_type=F32
    )
    return mixed.astype(BF).reshape(queries.shape), peak + jnp.log(total)


def attend_backward(queries, keys, values, grad_out, log_totals, mask):
    q, k, v, do = (split_heads(m) for m in (queries, keys, values, grad_out))
    scale = HEAD_DIM ** (-0.5)
    weights = jnp.exp(masked_scores(q, k, mask) - log_totals)
    grad_weights = jnp.einsum("qhd,khd->hqk", do, v, preferred_element_type=F32)
    grad_scores = (
        weights * (grad_weights - jnp.sum(weights * grad_weights, -1, keepdims=True))
    ).astype(BF)
    dq = jnp.einsum("hqk,khd->qhd", grad_scores, k, preferred_element_type=F32) * scale
    dk = jnp.einsum("hqk,qhd->khd", grad_scores, q, preferred_element_type=F32) * scale
    dv = jnp.einsum("hqk,qhd->khd", weights.astype(BF), do, preferred_element_type=F32)
    return tuple(m.astype(BF).reshape(queries.shape) for m in (dq, dk, dv))


def per_device(
    hidden_in,
    cotangent,
    norm_gain,
    norm_shift,
    inward,
    inward_bias,
    outward,
    outward_bias,
    expand,
    expand_bias,
    shrink,
    shrink_bias,
):
    stream = swap_halves(hidden_in).astype(F32)
    columns = inward.shape[3]
    w_in, w_out, w_up, w_down = [], [], [], []
    for layer in range(LAYERS):
        w_in.append(fetch_weights(inward[layer].reshape(-1, 3 * columns), 1))
        if layer == 0:
            biases = fetch_weights(
                jnp.concatenate([inward_bias.reshape(-1, 128), expand_bias.reshape(-1, 128)]), -1
            )
            bias_in = biases[:4].reshape(LAYERS, 2, columns)
            bias_up = biases[4:].reshape(LAYERS, -1)
        w_out.append(fetch_weights(outward[layer], -1))
        w_up.append(fetch_weights(expand[layer], -1))
        w_down.append(fetch_weights(shrink[layer], 1))
    cotangent = swap_halves(cotangent)

    places = row_places()
    mask = (places[:, None] >= places[None, :])[None]
    saved = []
    for layer in range(LAYERS):
        normed = layer_norm(stream, norm_gain[layer, 0], norm_shift[layer, 0]).astype(BF)
        normed_all = gather_rows(normed)
        projected = jnp.dot(normed_all, w_in[layer], preferred_element_type=F32)
        queries = (projected[:, :columns] + bias_in[layer, 0]).astype(BF)
        keys = projected[:, columns : 2 * columns].astype(BF)
        values = (projected[:, 2 * columns :] + bias_in[layer, 1]).astype(BF)
        attended, log_totals = attend_forward(queries, keys, values, mask)
        middle = stream + (
            scatter_rows(jnp.dot(attended, w_out[layer], preferred_element_type=F32))[0]
            + outward_bias[layer]
        )
        normed_mid = layer_norm(middle, norm_gain[layer, 1], norm_shift[layer, 1]).astype(BF)
        mid_all = gather_rows(normed_mid)
        hidden_pre = (
            jnp.dot(mid_all, w_up[layer], preferred_element_type=F32) + bias_up[layer]
        )
        activated = gelu_tanh(hidden_pre).astype(BF)
        result = middle + (
            scatter_rows(jnp.dot(activated, w_down[layer], preferred_element_type=F32))[0]
            + shrink_bias[layer]
        )
        saved.append(
            (stream, normed_all, queries, keys, values, attended, log_totals, middle, mid_all,
             hidden_pre, activated)
        )
        stream = result
    hidden_out = swap_halves(stream)

    grad_stream = cotangent.astype(F32)
    gains, shifts, sums_out, sums_down, sums_in, sums_up = {}, {}, {}, {}, {}, {}
    grads_mlp, grads_attn = [None] * LAYERS, [None] * LAYERS
    for layer in reversed(range(LAYERS)):
        (stream, normed_all, queries, keys, values, attended, log_totals, middle, mid_all,
         hidden_pre, activated) = saved[layer]
        dy = grad_stream.astype(BF)
        sums_down[layer] = jnp.sum(dy, 0, dtype=F32)
        dy_all = gather_rows(dy)
        grad_act = against_rows(dy_all, w_down[layer])
        du = jax.vjp(gelu_tanh, hidden_pre)[1](grad_act)[0].astype(BF)
        sums_up[layer] = jnp.sum(du, 0, dtype=F32)
        dh, sent = scatter_rows(against_rows(du, w_up[layer]))
        du, dy_all, sent = lax.optimization_barrier((du, dy_all, sent))
        grads_mlp[layer] = scatter_grads(
            jnp.stack(
                [tokens_inner(dy_all, activated).astype(BF), tokens_inner(mid_all, du).astype(BF)]
            )
        )
        back_mid = jax.vjp(layer_norm, middle, norm_gain[layer, 1], norm_shift[layer, 1])[1]
        grad_part, gains[layer, 1], shifts[layer, 1] = back_mid(dh)
        grad_middle = grad_stream + grad_part
        dz = grad_middle.astype(BF)
        sums_out[layer] = jnp.sum(dz, 0, dtype=F32)
        dz_all = gather_rows(dz)
        do = against_rows(dz_all, w_out[layer]).astype(BF)
        dq, dk, dv = attend_backward(queries, keys, values, do, log_totals, mask)
        sums_in[layer] = jnp.stack([jnp.sum(dq, 0, dtype=F32), jnp.sum(dv, 0, dtype=F32)])
        dqkv = jnp.concatenate([dq, dk, dv], 1)
        da, sent = scatter_rows(against_rows(dqkv, w_in[layer]))
        dqkv, dz_all, sent = lax.optimization_barrier((dqkv, dz_all, sent))
        grads_attn[layer] = scatter_grads(
            jnp.concatenate(
                [
                    tokens_inner(dz_all, attended).astype(BF),
                    tokens_inner(normed_all, dqkv).astype(BF),
                ],
                1,
            )[None]
        )
        back_in = jax.vjp(layer_norm, stream, norm_gain[layer, 0], norm_shift[layer, 0])[1]
        grad_first, gains[layer, 0], shifts[layer, 0] = back_in(da)
        grad_stream = grad_middle + grad_first
    grad_hidden = swap_halves(grad_stream)

    shard = lax.axis_index("c") * 4 + lax.axis_index("z")
    own = lax.axis_index("yl") * 4 + lax.axis_index("z")
    both = range(LAYERS)
    up = jnp.stack([sums_up[n] for n in both])[:, None]
    qv = jnp.stack([sums_in[n] for n in both])[:, :, None]
    up = lax.dynamic_update_slice_in_dim(jnp.zeros((LAYERS, 8, up.shape[2]), F32), up, shard, 1)
    qv = lax.dynamic_update_slice_in_dim(jnp.zeros((LAYERS, 2, 8, columns), F32), qv, shard, 2)
    vectors = jnp.concatenate(
        [
            m.reshape(-1, 128)
            for m in (
                [gains[n, i] for n in both for i in (0, 1)]
                + [shifts[n, i] for n in both for i in (0, 1)]
                + [sums_out[n] for n in both]
                + [sums_down[n] for n in both]
                + [up, qv]
            )
        ]
    )
    vectors = sum_everywhere(vectors)
    grad_gain = vectors[:32].reshape(LAYERS, 2, 1024)
    grad_shift = vectors[32:64].reshape(LAYERS, 2, 1024)
    grad_out_bias = vectors[64:80].reshape(LAYERS, 1024)
    grad_down_bias = vectors[80:96].reshape(LAYERS, 1024)
    up = vectors[96:160].reshape(LAYERS, 8, -1)
    qv = vectors[160:].reshape(LAYERS, 2, 8, columns)
    grad_up_bias = lax.dynamic_index_in_dim(up, own, 1, keepdims=False)
    grad_in_bias = lax.dynamic_index_in_dim(qv, own, 2, keepdims=False)

    return (
        hidden_out,
        grad_hidden,
        grad_gain,
        grad_shift,
        jnp.stack([g[0, :, columns:].reshape(-1, 3, columns) for g in grads_attn]),
        grad_in_bias,
        jnp.stack([g[0, :, :columns].T for g in grads_attn]),
        grad_out_bias,
        jnp.stack([g[1] for g in grads_mlp]),
        grad_up_bias,
        jnp.stack([g[0].T for g in grads_mlp]),
        grad_down_bias,
    )


def solution(mesh):
    fine = Mesh(mesh.devices.reshape(2, 4, 2, 2, 4), ("yh", "x", "c", "yl", "z"))
    dp, tensor = ("yh", "x", "c"), ("yl", "z")
    rows = P(dp + tensor, None)
    return jax.shard_map(
        per_device,
        mesh=fine,
        in_specs=(
            rows,
            rows,
            P(),
            P(),
            P(None, None, None, tensor),
            P(None, None, tensor),
            P(None, tensor, None),
            P(),
            P(None, None, tensor),
            P(None, tensor),
            P(None, tensor, None),
            P(),
        ),
        out_specs=(
            rows,
            rows,
            P(),
            P(),
            P(None, dp, None, tensor),
            P(None, None, tensor),
            P(None, tensor, dp),
            P(),
            P(None, dp, tensor),
            P(None, tensor),
            P(None, tensor, dp),
            P(),
        ),
        check_vma=False,
    )
```

```python
import jax
import jax.numpy as jnp
from jax import lax
from jax.experimental import pallas as pl
from jax.experimental.pallas import tpu as pltpu
from jax.sharding import Mesh
from jax.sharding import PartitionSpec as P

HEAD_DIM = 64
LAYERS = 2
EPS_NORM = 1e-05
NEG_FILL = -1000000000.0
BF = jnp.bfloat16
F32 = jnp.float32
RINGS = {"z": ("z",), "x": ("x",), "y": ("yh", "yl")}


def layer_norm(stream, norm_gain, norm_shift):
    center = stream - jnp.mean(stream, -1, keepdims=True)
    spread = jnp.mean(center * center, -1, keepdims=True)
    return center * lax.rsqrt(spread + EPS_NORM) * norm_gain + norm_shift


def gelu_tanh(values):
    return (
        0.5
        * values
        * (1.0 + jnp.tanh(0.7978845608028654 * (values + 0.044715 * values * values * values)))
    )


def tokens_inner(left, right):
    return lax.dot_general(left, right, (((0,), (0,)), ((), ())), preferred_element_type=F32)


def against_rows(left, right):
    return lax.dot_general(left, right, (((1,), (1,)), ((), ())), preferred_element_type=F32)


def ring(values, axis, step):
    return lax.ppermute(values, RINGS[axis], [(i, (i + step) % 4) for i in range(4)])


def swap_cores(values):
    return lax.ppermute(values, "c", [(0, 1), (1, 0)])


def swap_halves(values):
    return lax.ppermute(values, ("c", "yl"), [(0, 0), (1, 2), (2, 1), (3, 3)])


def y_pairs(rule):
    pairs = []
    for y in range(4):
        for core in range(2):
            target = rule(y, core)
            if target is not None:
                y2, core2 = target[0] % 4, target[1]
                pairs.append(
                    ((y // 2) * 4 + core * 2 + y % 2, (y2 // 2) * 4 + core2 * 2 + y2 % 2)
                )
    return pairs


def fetch_weights(values, step):
    return lax.ppermute(
        values,
        ("yh", "c", "yl"),
        y_pairs(lambda y, c: (y - step, y % 2) if c == y % 2 else (y, y % 2)),
    )


def after(token, *values):
    return lax.optimization_barrier((token,) + values)[1:]


def run_beside(token, chain, tasks):
    results = [task(*after(token, *operands)) for task, operands in tasks]
    return lax.optimization_barrier((chain, results))


def gather_ring(values, tasks=()):
    before = ring(values, "z", 1)
    behind = ring(values, "z", -1)
    across = ring(values, "z", 2)
    return run_beside(values, jnp.concatenate([values, before, behind, across]), tasks)


def gather_pair(mine):
    return jnp.concatenate([mine, swap_cores(mine)])


def gather_rows(values, tasks=()):
    mine, results = gather_ring(values, tasks)
    return gather_pair(mine), results


def scatter_pair(partial):
    half = partial.shape[0] // 2
    return partial[:half] + swap_cores(partial[half:].astype(BF)).astype(F32)


def scatter_rows(partial, tasks=()):
    both = scatter_pair(partial)
    low = both.astype(BF)
    rows = low.shape[0] // 4
    total = (
        both[:rows]
        + ring(low[rows : 2 * rows], "z", -1).astype(F32)
        + ring(low[2 * rows : 3 * rows], "z", 1).astype(F32)
        + ring(low[3 * rows :], "z", 2).astype(F32)
    )
    return run_beside(low, total, tasks)


def grad_blocks(pairs):
    place = lax.axis_index("x").astype(jnp.int32).reshape(1)
    tokens = pairs[0][0].shape[0]
    widths = [right.shape[1] for _, right in pairs]
    total = sum(widths)
    count = len(pairs)

    def kernel(place_ref, *refs):
        lefts, rights, outs = refs[: 2 * count], refs[2 * count : 3 * count], refs[3 * count :]
        step = pl.program_id(0)
        for d in range(4):

            @pl.when(step == d)
            def _():
                start = 0
                for i in range(count):
                    for high in range(2):
                        outs[d][high, :, start : start + widths[i]] = tokens_inner(
                            lefts[2 * i + high][...], rights[i][...]
                        ).astype(BF)
                    start += widths[i]

    def left_spec(high):
        return pl.BlockSpec((tokens, 128), lambda d, p: (0, high * 4 + lax.rem(p[0] + d, 4)))

    return pl.pallas_call(
        kernel,
        grid_spec=pltpu.PrefetchScalarGridSpec(
            num_scalar_prefetch=1,
            grid=(4,),
            in_specs=[left_spec(high) for _ in pairs for high in range(2)]
            + [pl.BlockSpec((tokens, width), lambda d, p: (0, 0)) for width in widths],
            out_specs=[pl.BlockSpec((2, 128, total), lambda d, p: (0, 0, 0))] * 4,
        ),
        out_shape=[jax.ShapeDtypeStruct((2, 128, total), BF)] * 4,
        compiler_params=pltpu.CompilerParams(vmem_limit_bytes=24 * 1024 * 1024),
        cost_estimate=pl.CostEstimate(
            flops=2 * tokens * 1024 * total, bytes_accessed=8 * 1024 * 1024, transcendentals=0
        ),
    )(place, *[left for left, _ in pairs for _ in range(2)], *[right for _, right in pairs])


def send_x(blocks):
    return blocks[0], ring(blocks[1], "x", 1), ring(blocks[3], "x", -1), ring(blocks[2], "x", 2)


def add_x(own, before, behind, across):
    summed = own.astype(F32) + before.astype(F32) + behind.astype(F32) + across.astype(F32)
    high, low_place = lax.axis_index("yh"), lax.axis_index("yl")
    y = high * 2 + low_place

    def pick(index):
        return jnp.where(index == 0, summed[0], summed[1])

    return (
        pick(high),
        pick(((y + 1) % 4) // 2).astype(BF),
        pick(((y + 3) % 4) // 2).astype(BF),
        pick(1 - high).astype(BF),
    )


def send_y(own, up, down, far):
    axes = ("yh", "c", "yl")
    return (
        own,
        lax.ppermute(up, axes, y_pairs(lambda y, c: (y + 1, c) if c != y % 2 else None)),
        lax.ppermute(down, axes, y_pairs(lambda y, c: (y + 3, c) if c != y % 2 else None)),
        lax.ppermute(far, axes, y_pairs(lambda y, c: (y + 2, c) if c == y % 2 else None)),
    )


def add_y(own, up, down, far):
    total = own + up.astype(F32) + down.astype(F32) + far.astype(F32)
    core = lax.axis_index("c")
    first, second = total[:64], total[64:]
    return jnp.where(core == 0, first, second), jnp.where(core == 0, second, first)


def send_core(keep, give):
    got = lax.ppermute(give, ("c", "yl"), [(0, 2), (3, 1)])
    return jnp.where(lax.axis_index("c") == lax.axis_index("yl"), keep, got)


def sum_everywhere(values):
    values = values + swap_cores(values)
    for axis in ("z", "x", "y"):
        values = (values + ring(values, axis, 2)) + (
            ring(values, axis, 1) + ring(values, axis, -1)
        )
    return values


def row_places():
    core, z = lax.axis_index("c"), lax.axis_index("z")
    blocks = jnp.stack([cc * 4 + (z + dz) % 4 for cc in (core, 1 - core) for dz in (0, 3, 1, 2)])
    return (blocks[:, None] * 128 + lax.iota(jnp.int32, 128)[None, :]).reshape(-1)


QUERY_ROWS = 256
VMEM_BYTES = 32 * 1024 * 1024


def attend_forward_kernel(query_place, key_place, q_ref, k_ref, v_ref, out_ref, log_ref):
    mask = query_place[...] >= key_place[...]
    for head in range(q_ref.shape[1] // HEAD_DIM):
        cut = slice(head * HEAD_DIM, (head + 1) * HEAD_DIM)
        scores = against_rows(k_ref[:, cut], q_ref[:, cut]) * HEAD_DIM ** (-0.5)
        scores = jnp.where(mask, scores, NEG_FILL)
        peak = jnp.max(scores, 0, keepdims=True)
        weights = jnp.exp(scores - peak)
        total = jnp.sum(weights, 0, keepdims=True)
        weights = (weights / total).astype(BF)
        out_ref[:, cut] = tokens_inner(v_ref[:, cut], weights).T.astype(BF)
        log_ref[head : head + 1, :] = peak + jnp.log(total)


def attend_forward(qkv, places):
    tokens, width = qkv.shape[0], qkv.shape[1] // 3
    heads = width // HEAD_DIM
    return pl.pallas_call(
        attend_forward_kernel,
        grid=(tokens // QUERY_ROWS,),
        in_specs=[
            pl.BlockSpec((1, QUERY_ROWS), lambda i: (0, i)),
            pl.BlockSpec((tokens, 1), lambda i: (0, 0)),
            pl.BlockSpec((QUERY_ROWS, width), lambda i: (i, 0)),
            pl.BlockSpec((tokens, width), lambda i: (0, 1)),
            pl.BlockSpec((tokens, width), lambda i: (0, 2)),
        ],
        out_specs=[
            pl.BlockSpec((QUERY_ROWS, width), lambda i: (i, 0)),
            pl.BlockSpec((heads, QUERY_ROWS), lambda i: (0, i)),
        ],
        out_shape=[
            jax.ShapeDtypeStruct((tokens, width), BF),
            jax.ShapeDtypeStruct((heads, tokens), F32),
        ],
        compiler_params=pltpu.CompilerParams(vmem_limit_bytes=VMEM_BYTES),
        cost_estimate=pl.CostEstimate(
            flops=8 * tokens * tokens * width, bytes_accessed=2 ** 21, transcendentals=tokens * tokens * heads
        ),
    )(places[None, :], places[:, None], qkv, qkv, qkv)


def attend_backward_kernel(
    query_place, key_place, log_ref, q_ref, k_ref, v_ref, do_ref, out_ref, dk_ref, dv_ref
):
    step = pl.program_id(0)
    width = q_ref.shape[1]
    rows = pl.ds(pl.multiple_of(step * QUERY_ROWS, QUERY_ROWS), QUERY_ROWS)
    mask = query_place[...] >= key_place[...]
    scale = HEAD_DIM ** (-0.5)

    @pl.when(step == 0)
    def _():
        dk_ref[...] = jnp.zeros_like(dk_ref)
        dv_ref[...] = jnp.zeros_like(dv_ref)

    for head in range(width // HEAD_DIM):
        cut = slice(head * HEAD_DIM, (head + 1) * HEAD_DIM)
        q, k, v, do = q_ref[:, cut], k_ref[:, cut], v_ref[:, cut], do_ref[:, cut]
        scores = jnp.where(mask, against_rows(k, q) * scale, NEG_FILL)
        weights = jnp.exp(scores - log_ref[head : head + 1, :])
        grad_weights = against_rows(v, do)
        mean = jnp.sum(weights * grad_weights, 0, keepdims=True)
        grad_scores = (weights * (grad_weights - mean)).astype(BF)
        out_ref[rows, cut] = (tokens_inner(k, grad_scores).T * scale).astype(BF)
        dk_ref[:, cut] += jnp.dot(grad_scores, q, preferred_element_type=F32)
        dv_ref[:, cut] += jnp.dot(weights.astype(BF), do, preferred_element_type=F32)

    @pl.when(step == pl.num_programs(0) - 1)
    def _():
        out_ref[:, width : 2 * width] = (dk_ref[...] * scale).astype(BF)
        out_ref[:, 2 * width :] = dv_ref[...].astype(BF)


def attend_backward(qkv, grad_out, log_totals, places):
    tokens, width = qkv.shape[0], qkv.shape[1] // 3
    heads = width // HEAD_DIM
    return pl.pallas_call(
        attend_backward_kernel,
        grid=(tokens // QUERY_ROWS,),
        in_specs=[
            pl.BlockSpec((1, QUERY_ROWS), lambda i: (0, i)),
            pl.BlockSpec((tokens, 1), lambda i: (0, 0)),
            pl.BlockSpec((heads, QUERY_ROWS), lambda i: (0, i)),
            pl.BlockSpec((QUERY_ROWS, width), lambda i: (i, 0)),
            pl.BlockSpec((tokens, width), lambda i: (0, 1)),
            pl.BlockSpec((tokens, width), lambda i: (0, 2)),
            pl.BlockSpec((QUERY_ROWS, width), lambda i: (i, 0)),
        ],
        out_specs=pl.BlockSpec((tokens, 3 * width), lambda i: (0, 0)),
        out_shape=jax.ShapeDtypeStruct((tokens, 3 * width), BF),
        scratch_shapes=[pltpu.VMEM((tokens, width), F32), pltpu.VMEM((tokens, width), F32)],
        compiler_params=pltpu.CompilerParams(vmem_limit_bytes=VMEM_BYTES),
        cost_estimate=pl.CostEstimate(
            flops=20 * tokens * tokens * width, bytes_accessed=2 ** 22, transcendentals=tokens * tokens * heads
        ),
    )(places[None, :], places[:, None], log_totals, qkv, qkv, qkv, grad_out)


def per_device(
    hidden_in,
    cotangent,
    norm_gain,
    norm_shift,
    inward,
    inward_bias,
    outward,
    outward_bias,
    expand,
    expand_bias,
    shrink,
    shrink_bias,
):
    stream = swap_halves(hidden_in).astype(F32)
    columns = inward.shape[3]
    w_in, w_out, w_up, w_down = [], [], [], []
    for layer in range(LAYERS):
        w_in.append(fetch_weights(inward[layer].reshape(-1, 3 * columns), 1))
        if layer == 0:
            biases = fetch_weights(
                jnp.concatenate([inward_bias.reshape(-1, 128), expand_bias.reshape(-1, 128)]), -1
            )
            bias_in = biases[:4].reshape(LAYERS, 2, columns)
            bias_up = biases[4:].reshape(LAYERS, -1)
        w_out.append(fetch_weights(outward[layer], -1))
        w_up.append(fetch_weights(expand[layer], -1))
        w_down.append(fetch_weights(shrink[layer], 1))
    cotangent = swap_halves(cotangent)

    places = row_places()
    saved = []
    pieces = {}

    def cotangent_task(step):
        def task(values):
            pieces[step] = ring(values, "z", step)
            return pieces[step]

        return [(task, (cotangent,))]

    for layer in range(LAYERS):
        normed = layer_norm(stream, norm_gain[layer, 0], norm_shift[layer, 0]).astype(BF)
        normed_all, _ = gather_rows(normed)
        qkv_bias = jnp.concatenate(
            [bias_in[layer, 0], jnp.zeros((columns,), F32), bias_in[layer, 1]]
        )
        qkv = (
            jnp.dot(normed_all, w_in[layer], preferred_element_type=F32) + qkv_bias
        ).astype(BF)
        attended, log_totals = attend_forward(qkv, places)
        attended, (piece,) = run_beside(
            normed_all, attended, cotangent_task(1 if layer == 0 else 2)
        )
        pieces[1 if layer == 0 else 2] = piece
        if layer == 1:
            attended, w_up[1], w_down[1] = lax.optimization_barrier(
                (attended, w_up[1], w_down[1])
            )
        middle = stream + (
            scatter_rows(jnp.dot(attended, w_out[layer], preferred_element_type=F32))[0]
            + outward_bias[layer]
        )
        normed_mid = layer_norm(middle, norm_gain[layer, 1], norm_shift[layer, 1]).astype(BF)
        if layer == 0:
            normed_mid, w_up[0], w_down[0] = lax.optimization_barrier(
                (normed_mid, w_up[0], w_down[0])
            )
        mid_mine, _ = gather_ring(normed_mid)
        mid_all = gather_pair(mid_mine)
        hidden_pre = (
            jnp.dot(mid_all, w_up[layer], preferred_element_type=F32) + bias_up[layer]
        )
        activated = gelu_tanh(hidden_pre).astype(BF)
        saved.append(
            (stream, normed_all, qkv, attended, log_totals, middle, mid_all, hidden_pre,
             activated)
        )
        if layer == 0:
            activated, (pieces[-1],) = run_beside(mid_mine, activated, cotangent_task(-1))
            activated, w_in[1], w_out[1] = lax.optimization_barrier(
                (activated, w_in[1], w_out[1])
            )
            stream = middle + (
                scatter_rows(jnp.dot(activated, w_down[layer], preferred_element_type=F32))[0]
                + shrink_bias[layer]
            )
    cotangent_ring = jnp.concatenate([cotangent, pieces[1], pieces[-1], pieces[2]])

    grad_stream = cotangent.astype(F32)
    gains, shifts, sums_out, sums_down, sums_in, sums_up = {}, {}, {}, {}, {}, {}
    grads_mlp, grads_attn = [None] * LAYERS, [None] * LAYERS

    _, normed_all, qkv, attended, log_totals, middle, mid_all, hidden_pre, activated = saved[1]
    sums_down[1] = jnp.sum(cotangent, 0, dtype=F32)
    dy_all = gather_pair(cotangent_ring)

    def mlp_back(layer, dy_all):
        hidden_pre = saved[layer][7]
        grad_act = against_rows(dy_all, w_down[layer])
        du = jax.vjp(gelu_tanh, hidden_pre)[1](grad_act)[0].astype(BF)
        return du

    def mlp_sum(layer, du, dy_all, tasks):
        _, _, _, _, _, middle, mid_all, hidden_pre, activated = saved[layer]
        sums_up[layer] = jnp.sum(du, 0, dtype=F32)

        def make(dy_all, activated, mid_all, du):
            return grad_blocks([(dy_all, activated), (mid_all, du)])

        dh, results = scatter_rows(
            against_rows(du, w_up[layer]), [(make, (dy_all, activated, mid_all, du))] + tasks
        )
        back_mid = jax.vjp(layer_norm, middle, norm_gain[layer, 1], norm_shift[layer, 1])[1]
        grad_part, gains[layer, 1], shifts[layer, 1] = back_mid(dh)
        return grad_part, results

    def attn_sum(layer, dqkv, dz_all, tasks):
        stream, normed_all, _, attended, _, _, _, _, _ = saved[layer]
        sums = jnp.sum(dqkv, 0, dtype=F32)
        sums_in[layer] = jnp.stack([sums[:columns], sums[2 * columns :]])

        def make(dz_all, attended, normed_all, dqkv):
            return grad_blocks([(dz_all, attended), (normed_all, dqkv)])

        da, results = scatter_rows(
            against_rows(dqkv, w_in[layer]), [(make, (dz_all, attended, normed_all, dqkv))] + tasks
        )
        back_in = jax.vjp(layer_norm, stream, norm_gain[layer, 0], norm_shift[layer, 0])[1]
        grad_first, gains[layer, 0], shifts[layer, 0] = back_in(da)
        return grad_first, results

    du = mlp_back(1, dy_all)
    grad_part, (mlp1,) = mlp_sum(1, du, dy_all, [])
    grad_middle = grad_stream + grad_part
    mlp1 = send_x(mlp1)
    dz = grad_middle.astype(BF)
    sums_out[1] = jnp.sum(dz, 0, dtype=F32)
    dz_all, _ = gather_rows(dz)
    do = against_rows(dz_all, w_out[1]).astype(BF)
    dqkv = attend_backward(qkv, do, log_totals, places)

    def last_pairs(activated):
        both = scatter_pair(jnp.dot(activated, w_down[1], preferred_element_type=F32))
        low = both.astype(BF)
        rows = low.shape[0] // 4
        near = (
            both[:rows]
            + ring(low[rows : 2 * rows], "z", -1).astype(F32)
            + ring(low[2 * rows : 3 * rows], "z", 1).astype(F32)
        )
        return near, low[3 * rows :]

    dqkv, ((last_near, last_far),) = run_beside(dz_all, dqkv, [(last_pairs, (activated,))])
    grad_first, (attn1, mlp1) = attn_sum(1, dqkv, dz_all, [(add_x, mlp1)])
    grad_stream = grad_middle + grad_first
    attn1, mlp1 = send_x(attn1), send_y(*mlp1)

    _, normed_all, qkv, attended, log_totals, middle, mid_all, hidden_pre, activated = saved[0]
    dy = grad_stream.astype(BF)
    sums_down[0] = jnp.sum(dy, 0, dtype=F32)
    dy_mine, (mlp1,) = gather_ring(dy, [(add_y, mlp1)])
    grads_mlp[1] = send_core(*mlp1)
    dy_all = gather_pair(dy_mine)
    du = mlp_back(0, dy_all)
    du, (last_across,) = run_beside(
        dy_mine, du, [(lambda values: ring(values, "z", 2), (last_far,))]
    )
    hidden_out = swap_halves(
        saved[1][5] + (last_near + last_across.astype(F32) + shrink_bias[1])
    )
    grad_part, (mlp0, attn1) = mlp_sum(0, du, dy_all, [(add_x, attn1)])
    grad_middle = grad_stream + grad_part
    mlp0, attn1 = send_x(mlp0), send_y(*attn1)
    dz = grad_middle.astype(BF)
    sums_out[0] = jnp.sum(dz, 0, dtype=F32)
    dz_all, (attn1,) = gather_rows(dz, [(add_y, attn1)])
    grads_attn[1] = send_core(*attn1)
    do = against_rows(dz_all, w_out[0]).astype(BF)
    dqkv = attend_backward(qkv, do, log_totals, places)
    grad_first, (attn0, mlp0) = attn_sum(0, dqkv, dz_all, [(add_x, mlp0)])
    grad_stream = grad_middle + grad_first
    grad_hidden = swap_halves(grad_stream)
    attn0 = add_x(*send_x(attn0))
    grads_mlp[0] = send_core(*add_y(*send_y(*mlp0)))
    grads_attn[0] = send_core(*add_y(*send_y(*attn0)))

    shard = lax.axis_index("c") * 4 + lax.axis_index("z")
    own = lax.axis_index("yl") * 4 + lax.axis_index("z")
    both = range(LAYERS)
    up = jnp.stack([sums_up[n] for n in both])[:, None]
    qv = jnp.stack([sums_in[n] for n in both])[:, :, None]
    up = lax.dynamic_update_slice_in_dim(jnp.zeros((LAYERS, 8, up.shape[2]), F32), up, shard, 1)
    qv = lax.dynamic_update_slice_in_dim(jnp.zeros((LAYERS, 2, 8, columns), F32), qv, shard, 2)
    vectors = jnp.concatenate(
        [
            m.reshape(-1, 128)
            for m in (
                [gains[n, i] for n in both for i in (0, 1)]
                + [shifts[n, i] for n in both for i in (0, 1)]
                + [sums_out[n] for n in both]
                + [sums_down[n] for n in both]
                + [up, qv]
            )
        ]
    )
    vectors = sum_everywhere(vectors)
    grad_gain = vectors[:32].reshape(LAYERS, 2, 1024)
    grad_shift = vectors[32:64].reshape(LAYERS, 2, 1024)
    grad_out_bias = vectors[64:80].reshape(LAYERS, 1024)
    grad_down_bias = vectors[80:96].reshape(LAYERS, 1024)
    up = vectors[96:160].reshape(LAYERS, 8, -1)
    qv = vectors[160:].reshape(LAYERS, 2, 8, columns)
    grad_up_bias = lax.dynamic_index_in_dim(up, own, 1, keepdims=False)
    grad_in_bias = lax.dynamic_index_in_dim(qv, own, 2, keepdims=False)

    width = shrink.shape[1]
    return (
        hidden_out,
        grad_hidden,
        grad_gain,
        grad_shift,
        jnp.stack([g[:, columns:].reshape(-1, 3, columns) for g in grads_attn]),
        grad_in_bias,
        jnp.stack([g[:, :columns].T for g in grads_attn]),
        grad_out_bias,
        jnp.stack([g[:, width:] for g in grads_mlp]),
        grad_up_bias,
        jnp.stack([g[:, :width].T for g in grads_mlp]),
        grad_down_bias,
    )


def solution(mesh):
    fine = Mesh(mesh.devices.reshape(2, 4, 2, 2, 4), ("yh", "x", "c", "yl", "z"))
    dp, tensor = ("yh", "x", "c"), ("yl", "z")
    rows = P(dp + tensor, None)
    return jax.shard_map(
        per_device,
        mesh=fine,
        in_specs=(
            rows,
            rows,
            P(),
            P(),
            P(None, None, None, tensor),
            P(None, None, tensor),
            P(None, tensor, None),
            P(),
            P(None, None, tensor),
            P(None, tensor),
            P(None, tensor, None),
            P(),
        ),
        out_specs=(
            rows,
            rows,
            P(),
            P(),
            P(None, dp, None, tensor),
            P(None, None, tensor),
            P(None, tensor, dp),
            P(),
            P(None, dp, tensor),
            P(None, tensor),
            P(None, tensor, dp),
            P(),
        ),
        check_vma=False,
    )
```

```python
import jax
import jax.numpy as jnp
from jax import lax
from jax.experimental import pallas as pl
from jax.experimental.pallas import tpu as pltpu
from jax.sharding import Mesh
from jax.sharding import PartitionSpec as P

HEAD_DIM = 64
LAYERS = 2
EPS_NORM = 1e-05
NEG_FILL = -1000000000.0
BF = jnp.bfloat16
F32 = jnp.float32
RINGS = {"z": ("z",), "x": ("x",), "y": ("yh", "yl")}


def layer_norm(stream, norm_gain, norm_shift):
    center = stream - jnp.mean(stream, -1, keepdims=True)
    spread = jnp.mean(center * center, -1, keepdims=True)
    return center * lax.rsqrt(spread + EPS_NORM) * norm_gain + norm_shift


def gelu_tanh(values):
    return (
        0.5
        * values
        * (1.0 + jnp.tanh(0.7978845608028654 * (values + 0.044715 * values * values * values)))
    )


def tokens_inner(left, right):
    return lax.dot_general(left, right, (((0,), (0,)), ((), ())), preferred_element_type=F32)


def against_rows(left, right):
    return lax.dot_general(left, right, (((1,), (1,)), ((), ())), preferred_element_type=F32)


def ring(values, axis, step):
    return lax.ppermute(values, RINGS[axis], [(i, (i + step) % 4) for i in range(4)])


def swap_cores(values):
    return lax.ppermute(values, "c", [(0, 1), (1, 0)])


def swap_halves(values):
    return lax.ppermute(values, ("c", "yl"), [(0, 0), (1, 2), (2, 1), (3, 3)])


def y_pairs(rule):
    pairs = []
    for y in range(4):
        for core in range(2):
            target = rule(y, core)
            if target is not None:
                y2, core2 = target[0] % 4, target[1]
                pairs.append(
                    ((y // 2) * 4 + core * 2 + y % 2, (y2 // 2) * 4 + core2 * 2 + y2 % 2)
                )
    return pairs


def fetch_weights(values, step):
    return lax.ppermute(
        values,
        ("yh", "c", "yl"),
        y_pairs(lambda y, c: (y - step, y % 2) if c == y % 2 else (y, y % 2)),
    )


def after(token, *values):
    return lax.optimization_barrier((token,) + values)[1:]


def run_beside(token, chain, tasks):
    results = [task(*after(token, *operands)) for task, operands in tasks]
    return lax.optimization_barrier((chain, results))


def gather_ring(values, tasks=()):
    before = ring(values, "z", 1)
    behind = ring(values, "z", -1)
    across = ring(values, "z", 2)
    return run_beside(values, jnp.concatenate([values, before, behind, across]), tasks)


def gather_pair(mine):
    return jnp.concatenate([mine, swap_cores(mine)])


def gather_rows(values, tasks=()):
    mine, results = gather_ring(values, tasks)
    return gather_pair(mine), results


def scatter_pair(left, product):
    half = left.shape[0] // 2
    other = swap_cores(product(left[half:]).astype(BF))
    return product(left[:half]) + other.astype(F32)


def scatter_rows(left, product, tasks=()):
    both = scatter_pair(left, product)
    low = both.astype(BF)
    rows = low.shape[0] // 4
    total = (
        both[:rows]
        + ring(low[rows : 2 * rows], "z", -1).astype(F32)
        + ring(low[2 * rows : 3 * rows], "z", 1).astype(F32)
        + ring(low[3 * rows :], "z", 2).astype(F32)
    )
    return run_beside(low, total, tasks)


def times(weight):
    return lambda left: jnp.dot(left, weight, preferred_element_type=F32)


def times_rows(weight):
    return lambda left: against_rows(left, weight)


def grad_blocks(pairs):
    place = lax.axis_index("x").astype(jnp.int32).reshape(1)
    tokens = pairs[0][0].shape[0]
    widths = [right.shape[1] for _, right in pairs]
    total = sum(widths)
    count = len(pairs)

    def kernel(place_ref, *refs):
        lefts, rights, outs = refs[: 2 * count], refs[2 * count : 3 * count], refs[3 * count :]
        step = pl.program_id(0)
        for d in range(4):

            @pl.when(step == d)
            def _():
                start = 0
                for i in range(count):
                    for high in range(2):
                        outs[d][high, :, start : start + widths[i]] = tokens_inner(
                            lefts[2 * i + high][...], rights[i][...]
                        ).astype(BF)
                    start += widths[i]

    def left_spec(high):
        return pl.BlockSpec((tokens, 128), lambda d, p: (0, high * 4 + lax.rem(p[0] + d, 4)))

    return pl.pallas_call(
        kernel,
        grid_spec=pltpu.PrefetchScalarGridSpec(
            num_scalar_prefetch=1,
            grid=(4,),
            in_specs=[left_spec(high) for _ in pairs for high in range(2)]
            + [pl.BlockSpec((tokens, width), lambda d, p: (0, 0)) for width in widths],
            out_specs=[pl.BlockSpec((2, 128, total), lambda d, p: (0, 0, 0))] * 4,
        ),
        out_shape=[jax.ShapeDtypeStruct((2, 128, total), BF)] * 4,
        compiler_params=pltpu.CompilerParams(vmem_limit_bytes=24 * 1024 * 1024),
        cost_estimate=pl.CostEstimate(
            flops=2 * tokens * 1024 * total, bytes_accessed=8 * 1024 * 1024, transcendentals=0
        ),
    )(place, *[left for left, _ in pairs for _ in range(2)], *[right for _, right in pairs])


def send_x(blocks):
    return blocks[0], ring(blocks[1], "x", 1), ring(blocks[3], "x", -1), ring(blocks[2], "x", 2)


def add_x(own, before, behind, across):
    summed = own.astype(F32) + before.astype(F32) + behind.astype(F32) + across.astype(F32)
    high, low_place = lax.axis_index("yh"), lax.axis_index("yl")
    y = high * 2 + low_place

    def pick(index):
        return jnp.where(index == 0, summed[0], summed[1])

    return (
        pick(high),
        pick(((y + 1) % 4) // 2).astype(BF),
        pick(((y + 3) % 4) // 2).astype(BF),
        pick(1 - high).astype(BF),
    )


def send_y(own, up, down, far):
    axes = ("yh", "c", "yl")
    return (
        own,
        lax.ppermute(up, axes, y_pairs(lambda y, c: (y + 1, c) if c != y % 2 else None)),
        lax.ppermute(down, axes, y_pairs(lambda y, c: (y + 3, c) if c != y % 2 else None)),
        lax.ppermute(far, axes, y_pairs(lambda y, c: (y + 2, c) if c == y % 2 else None)),
    )


def add_y(own, up, down, far):
    total = own + up.astype(F32) + down.astype(F32) + far.astype(F32)
    core = lax.axis_index("c")
    first, second = total[:64], total[64:]
    return jnp.where(core == 0, first, second), jnp.where(core == 0, second, first)


def send_core(keep, give):
    got = lax.ppermute(give, ("c", "yl"), [(0, 2), (3, 1)])
    return jnp.where(lax.axis_index("c") == lax.axis_index("yl"), keep, got)


def sum_everywhere(common, shard, steps, state):
    rows = common.shape[0]
    values = common
    for axis, step in zip(("z", "x", "y"), steps):
        if axis == "x":
            values = jnp.concatenate([values, shard])
        values = (values + ring(values, axis, 2)) + (
            ring(values, axis, 1) + ring(values, axis, -1)
        )
        values, state = lax.optimization_barrier((values, state))
        state = step(*state)
    other = swap_cores(values)
    own = lax.axis_index("c") == lax.axis_index("yl")
    return values[:rows] + other[:rows], jnp.where(own, values[rows:], other[rows:]), state


def row_places():
    core, z = lax.axis_index("c"), lax.axis_index("z")
    blocks = jnp.stack([cc * 4 + (z + dz) % 4 for cc in (core, 1 - core) for dz in (0, 3, 1, 2)])
    return (blocks[:, None] * 128 + lax.iota(jnp.int32, 128)[None, :]).reshape(-1)


QUERY_ROWS = 256
VMEM_BYTES = 32 * 1024 * 1024


def attend_forward_kernel(query_place, key_place, q_ref, k_ref, v_ref, out_ref, log_ref):
    mask = query_place[...] >= key_place[...]
    for head in range(q_ref.shape[1] // HEAD_DIM):
        cut = slice(head * HEAD_DIM, (head + 1) * HEAD_DIM)
        scores = against_rows(k_ref[:, cut], q_ref[:, cut] * HEAD_DIM ** (-0.5))
        scores = jnp.where(mask, scores, NEG_FILL)
        peak = jnp.max(scores, 0, keepdims=True)
        weights = jnp.exp(scores - peak)
        total = jnp.sum(weights, 0, keepdims=True)
        weights = (weights * (1.0 / total)).astype(BF)
        out_ref[:, cut] = tokens_inner(v_ref[:, cut], weights).T.astype(BF)
        log_ref[head : head + 1, :] = peak + jnp.log(total)


def attend_forward(qkv, places):
    tokens, width = qkv.shape[0], qkv.shape[1] // 3
    heads = width // HEAD_DIM
    return pl.pallas_call(
        attend_forward_kernel,
        grid=(tokens // QUERY_ROWS,),
        in_specs=[
            pl.BlockSpec((1, QUERY_ROWS), lambda i: (0, i)),
            pl.BlockSpec((tokens, 1), lambda i: (0, 0)),
            pl.BlockSpec((QUERY_ROWS, width), lambda i: (i, 0)),
            pl.BlockSpec((tokens, width), lambda i: (0, 1)),
            pl.BlockSpec((tokens, width), lambda i: (0, 2)),
        ],
        out_specs=[
            pl.BlockSpec((QUERY_ROWS, width), lambda i: (i, 0)),
            pl.BlockSpec((heads, QUERY_ROWS), lambda i: (0, i)),
        ],
        out_shape=[
            jax.ShapeDtypeStruct((tokens, width), BF),
            jax.ShapeDtypeStruct((heads, tokens), F32),
        ],
        compiler_params=pltpu.CompilerParams(vmem_limit_bytes=VMEM_BYTES),
        cost_estimate=pl.CostEstimate(
            flops=8 * tokens * tokens * width, bytes_accessed=2 ** 21, transcendentals=tokens * tokens * heads
        ),
    )(places[None, :], places[:, None], qkv, qkv, qkv)


def attend_backward_kernel(
    query_place, key_place, log_ref, q_ref, k_ref, v_ref, do_ref, out_ref, dk_ref, dv_ref
):
    step = pl.program_id(0)
    width = q_ref.shape[1]
    rows = pl.ds(pl.multiple_of(step * QUERY_ROWS, QUERY_ROWS), QUERY_ROWS)
    mask = query_place[...] >= key_place[...]
    scale = HEAD_DIM ** (-0.5)

    @pl.when(step == 0)
    def _():
        dk_ref[...] = jnp.zeros_like(dk_ref)
        dv_ref[...] = jnp.zeros_like(dv_ref)

    for head in range(width // HEAD_DIM):
        cut = slice(head * HEAD_DIM, (head + 1) * HEAD_DIM)
        q, k, v, do = q_ref[:, cut] * scale, k_ref[:, cut], v_ref[:, cut], do_ref[:, cut]
        scores = jnp.where(mask, against_rows(k, q), NEG_FILL)
        weights = jnp.exp(scores - log_ref[head : head + 1, :])
        grad_weights = against_rows(v, do)
        mean = jnp.sum(weights * grad_weights, 0, keepdims=True)
        grad_scores = (weights * (grad_weights - mean)).astype(BF)
        out_ref[rows, cut] = (tokens_inner(k, grad_scores).T * scale).astype(BF)
        dk_ref[:, cut] += jnp.dot(grad_scores, q, preferred_element_type=F32)
        dv_ref[:, cut] += jnp.dot(weights.astype(BF), do, preferred_element_type=F32)

    @pl.when(step == pl.num_programs(0) - 1)
    def _():
        out_ref[:, width : 2 * width] = dk_ref[...].astype(BF)
        out_ref[:, 2 * width :] = dv_ref[...].astype(BF)


def attend_backward(qkv, grad_out, log_totals, places):
    tokens, width = qkv.shape[0], qkv.shape[1] // 3
    heads = width // HEAD_DIM
    return pl.pallas_call(
        attend_backward_kernel,
        grid=(tokens // QUERY_ROWS,),
        in_specs=[
            pl.BlockSpec((1, QUERY_ROWS), lambda i: (0, i)),
            pl.BlockSpec((tokens, 1), lambda i: (0, 0)),
            pl.BlockSpec((heads, QUERY_ROWS), lambda i: (0, i)),
            pl.BlockSpec((QUERY_ROWS, width), lambda i: (i, 0)),
            pl.BlockSpec((tokens, width), lambda i: (0, 1)),
            pl.BlockSpec((tokens, width), lambda i: (0, 2)),
            pl.BlockSpec((QUERY_ROWS, width), lambda i: (i, 0)),
        ],
        out_specs=pl.BlockSpec((tokens, 3 * width), lambda i: (0, 0)),
        out_shape=jax.ShapeDtypeStruct((tokens, 3 * width), BF),
        scratch_shapes=[pltpu.VMEM((tokens, width), F32), pltpu.VMEM((tokens, width), F32)],
        compiler_params=pltpu.CompilerParams(vmem_limit_bytes=VMEM_BYTES),
        cost_estimate=pl.CostEstimate(
            flops=20 * tokens * tokens * width, bytes_accessed=2 ** 22, transcendentals=tokens * tokens * heads
        ),
    )(places[None, :], places[:, None], log_totals, qkv, qkv, qkv, grad_out)


def per_device(
    hidden_in,
    cotangent,
    norm_gain,
    norm_shift,
    inward,
    inward_bias,
    outward,
    outward_bias,
    expand,
    expand_bias,
    shrink,
    shrink_bias,
):
    stream = swap_halves(hidden_in).astype(F32)
    columns = inward.shape[3]
    w_in, w_out, w_up, w_down = [], [], [], []
    for layer in range(LAYERS):
        w_in.append(fetch_weights(inward[layer].reshape(-1, 3 * columns), 1))
        if layer == 0:
            biases = fetch_weights(
                jnp.concatenate([inward_bias.reshape(-1, 128), expand_bias.reshape(-1, 128)]), -1
            )
            bias_in = biases[:4].reshape(LAYERS, 2, columns)
            bias_up = biases[4:].reshape(LAYERS, -1)
        w_out.append(fetch_weights(outward[layer], -1))
        w_up.append(fetch_weights(expand[layer], -1))
        w_down.append(fetch_weights(shrink[layer], 1))
    cotangent = swap_halves(cotangent)

    places = row_places()
    saved = []
    pieces = {}

    def cotangent_task(step):
        def task(values):
            pieces[step] = ring(values, "z", step)
            return pieces[step]

        return [(task, (cotangent,))]

    for layer in range(LAYERS):
        normed = layer_norm(stream, norm_gain[layer, 0], norm_shift[layer, 0]).astype(BF)
        mine, _ = gather_ring(normed)
        if layer == 1:
            mine, w_up[1], w_down[1] = lax.optimization_barrier((mine, w_up[1], w_down[1]))
        normed_all = gather_pair(mine)
        if layer == 0:
            normed_all, w_up[0] = lax.optimization_barrier((normed_all, w_up[0]))
        qkv_bias = jnp.concatenate(
            [bias_in[layer, 0], jnp.zeros((columns,), F32), bias_in[layer, 1]]
        )
        qkv = (
            jnp.dot(normed_all, w_in[layer], preferred_element_type=F32) + qkv_bias
        ).astype(BF)
        attended, log_totals = attend_forward(qkv, places)
        attended, (piece,) = run_beside(
            normed_all, attended, cotangent_task(1 if layer == 0 else 2)
        )
        pieces[1 if layer == 0 else 2] = piece
        if layer == 0:
            attended, w_down[0] = lax.optimization_barrier((attended, w_down[0]))
        middle = stream + (
            scatter_rows(attended, times(w_out[layer]))[0]
            + outward_bias[layer]
        )
        normed_mid = layer_norm(middle, norm_gain[layer, 1], norm_shift[layer, 1]).astype(BF)
        mid_mine, _ = gather_ring(normed_mid)
        if layer == 0:
            mid_mine, w_in[1], w_out[1] = lax.optimization_barrier((mid_mine, w_in[1], w_out[1]))
        mid_all = gather_pair(mid_mine)
        hidden_pre = (
            jnp.dot(mid_all, w_up[layer], preferred_element_type=F32) + bias_up[layer]
        )
        activated = gelu_tanh(hidden_pre).astype(BF)
        saved.append(
            (stream, normed_all, qkv, attended, log_totals, middle, mid_all, hidden_pre,
             activated)
        )
        if layer == 0:
            activated, (pieces[-1],) = run_beside(mid_mine, activated, cotangent_task(-1))
            stream = middle + (
                scatter_rows(activated, times(w_down[layer]))[0]
                + shrink_bias[layer]
            )
    cotangent_ring = jnp.concatenate([cotangent, pieces[1], pieces[-1], pieces[2]])

    grad_stream = cotangent.astype(F32)
    gains, shifts, sums_out, sums_down, sums_in, sums_up = {}, {}, {}, {}, {}, {}
    grads_mlp, grads_attn = [None] * LAYERS, [None] * LAYERS

    _, normed_all, qkv, attended, log_totals, middle, mid_all, hidden_pre, activated = saved[1]
    sums_down[1] = jnp.sum(cotangent, 0, dtype=F32)
    dy_all = gather_pair(cotangent_ring)

    def mlp_back(layer, dy_all):
        hidden_pre = saved[layer][7]
        grad_act = against_rows(dy_all, w_down[layer])
        du = jax.vjp(gelu_tanh, hidden_pre)[1](grad_act)[0].astype(BF)
        return du

    def mlp_sum(layer, du, dy_all, tasks):
        _, _, _, _, _, middle, mid_all, hidden_pre, activated = saved[layer]
        sums_up[layer] = jnp.sum(du, 0, dtype=F32)

        def make(dy_all, activated, mid_all, du):
            return grad_blocks([(dy_all, activated), (mid_all, du)])

        dh, results = scatter_rows(
            du, times_rows(w_up[layer]), [(make, (dy_all, activated, mid_all, du))] + tasks
        )
        back_mid = jax.vjp(layer_norm, middle, norm_gain[layer, 1], norm_shift[layer, 1])[1]
        grad_part, gains[layer, 1], shifts[layer, 1] = back_mid(dh)
        return grad_part, results

    def attn_sum(layer, dqkv, dz_all, tasks):
        stream, normed_all, _, attended, _, _, _, _, _ = saved[layer]
        sums = jnp.sum(dqkv, 0, dtype=F32)
        sums_in[layer] = jnp.stack([sums[:columns], sums[2 * columns :]])

        def make(dz_all, attended, normed_all, dqkv):
            return grad_blocks([(dz_all, attended), (normed_all, dqkv)])

        da, results = scatter_rows(
            dqkv, times_rows(w_in[layer]), [(make, (dz_all, attended, normed_all, dqkv))] + tasks
        )
        back_in = jax.vjp(layer_norm, stream, norm_gain[layer, 0], norm_shift[layer, 0])[1]
        grad_first, gains[layer, 0], shifts[layer, 0] = back_in(da)
        return grad_first, results

    du = mlp_back(1, dy_all)
    grad_part, (mlp1,) = mlp_sum(1, du, dy_all, [])
    grad_middle = grad_stream + grad_part
    mlp1 = send_x(mlp1)
    dz = grad_middle.astype(BF)
    sums_out[1] = jnp.sum(dz, 0, dtype=F32)
    dz_mine, _ = gather_ring(dz)
    dz_mine, near1 = lax.optimization_barrier((dz_mine, mlp1[:3]))
    dz_all = gather_pair(dz_mine)
    do = against_rows(dz_all, w_out[1]).astype(BF)
    dqkv = attend_backward(qkv, do, log_totals, places)

    def last_pairs(activated):
        both = scatter_pair(activated, times(w_down[1]))
        low = both.astype(BF)
        rows = low.shape[0] // 4
        near = (
            both[:rows]
            + ring(low[rows : 2 * rows], "z", -1).astype(F32)
            + ring(low[2 * rows : 3 * rows], "z", 1).astype(F32)
        )
        return near, low[3 * rows :]

    dqkv, ((last_near, last_far),) = run_beside(dz_all, dqkv, [(last_pairs, (activated,))])
    dqkv, mlp1 = lax.optimization_barrier((dqkv, (*near1, mlp1[3])))
    mlp1 = send_y(*add_x(*mlp1))
    grad_first, (attn1, mlp1) = attn_sum(1, dqkv, dz_all, [(add_y, mlp1)])
    grad_stream = grad_middle + grad_first
    attn1 = send_x(attn1)
    grads_mlp[1] = send_core(*mlp1)

    _, normed_all, qkv, attended, log_totals, middle, mid_all, hidden_pre, activated = saved[0]
    dy = grad_stream.astype(BF)
    sums_down[0] = jnp.sum(dy, 0, dtype=F32)
    dy_mine, _ = gather_ring(dy)
    dy_mine, attn1 = lax.optimization_barrier((dy_mine, attn1))
    attn1 = send_y(*add_x(*attn1))
    dy_all = gather_pair(dy_mine)
    du = mlp_back(0, dy_all)
    du, (last_across,) = run_beside(
        dy_mine, du, [(lambda values: ring(values, "z", 2), (last_far,))]
    )
    hidden_out = saved[1][5] + (last_near + last_across.astype(F32) + shrink_bias[1])
    hidden_out = swap_halves(hidden_out.astype(BF)).astype(F32)
    du, attn1 = lax.optimization_barrier((du, attn1))
    grad_part, (mlp0, attn1) = mlp_sum(0, du, dy_all, [(add_y, attn1)])
    grad_middle = grad_stream + grad_part
    mlp0 = send_x(mlp0)
    grads_attn[1] = send_core(*attn1)
    dz = grad_middle.astype(BF)
    sums_out[0] = jnp.sum(dz, 0, dtype=F32)
    dz_mine, _ = gather_ring(dz)
    dz_mine, near0 = lax.optimization_barrier((dz_mine, mlp0[:3]))
    dz_all = gather_pair(dz_mine)
    do = against_rows(dz_all, w_out[0]).astype(BF)
    dqkv = attend_backward(qkv, do, log_totals, places)
    dqkv, mlp0 = lax.optimization_barrier((dqkv, (*near0, mlp0[3])))
    mlp0 = send_y(*add_x(*mlp0))
    grad_first, (attn0, mlp0) = attn_sum(0, dqkv, dz_all, [(add_y, mlp0)])
    grad_stream = grad_middle + grad_first
    grad_hidden = swap_halves(grad_stream.astype(BF)).astype(F32)
    grads_mlp[0] = send_core(*mlp0)

    both = range(LAYERS)
    common = jnp.concatenate(
        [
            m.reshape(-1, 128)
            for m in (
                [gains[n, i] for n in both for i in (0, 1)]
                + [shifts[n, i] for n in both for i in (0, 1)]
                + [sums_out[n] for n in both]
                + [sums_down[n] for n in both]
            )
        ]
    )
    shard = jnp.concatenate(
        [m.reshape(-1, 128) for m in [sums_up[n] for n in both] + [sums_in[n] for n in both]]
    )
    common, shard, grads_attn[0] = sum_everywhere(
        common,
        shard,
        (
            lambda *m: m,
            lambda *m: send_y(*add_x(*m)),
            lambda *m: send_core(*add_y(*m)),
        ),
        send_x(attn0),
    )
    grad_gain = common[:32].reshape(LAYERS, 2, 1024)
    grad_shift = common[32:64].reshape(LAYERS, 2, 1024)
    grad_out_bias = common[64:80].reshape(LAYERS, 1024)
    grad_down_bias = common[80:96].reshape(LAYERS, 1024)
    grad_up_bias = shard[:8].reshape(LAYERS, -1)
    grad_in_bias = shard[8:].reshape(LAYERS, 2, columns)

    width = shrink.shape[1]
    return (
        hidden_out,
        grad_hidden,
        grad_gain,
        grad_shift,
        jnp.stack([g[:, columns:].reshape(-1, 3, columns) for g in grads_attn]),
        grad_in_bias,
        jnp.stack([g[:, :columns].T for g in grads_attn]),
        grad_out_bias,
        jnp.stack([g[:, width:] for g in grads_mlp]),
        grad_up_bias,
        jnp.stack([g[:, :width].T for g in grads_mlp]),
        grad_down_bias,
    )


def solution(mesh):
    fine = Mesh(mesh.devices.reshape(2, 4, 2, 2, 4), ("yh", "x", "c", "yl", "z"))
    dp, tensor = ("yh", "x", "c"), ("yl", "z")
    rows = P(dp + tensor, None)
    return jax.shard_map(
        per_device,
        mesh=fine,
        in_specs=(
            rows,
            rows,
            P(),
            P(),
            P(None, None, None, tensor),
            P(None, None, tensor),
            P(None, tensor, None),
            P(),
            P(None, None, tensor),
            P(None, tensor),
            P(None, tensor, None),
            P(),
        ),
        out_specs=(
            rows,
            rows,
            P(),
            P(),
            P(None, dp, None, tensor),
            P(None, None, tensor),
            P(None, tensor, dp),
            P(),
            P(None, dp, tensor),
            P(None, tensor),
            P(None, tensor, dp),
            P(),
        ),
        check_vma=False,
    )
```

```python
import jax
import jax.numpy as jnp
from jax import lax
from jax.experimental import pallas as pl
from jax.experimental.pallas import tpu as pltpu
from jax.sharding import Mesh
from jax.sharding import PartitionSpec as P

HEAD_DIM = 64
LAYERS = 2
EPS_NORM = 1e-05
NEG_FILL = -1000000000.0
BF = jnp.bfloat16
F32 = jnp.float32
RINGS = {"z": ("z",), "x": ("x",), "y": ("yh", "yl")}


def layer_norm(stream, norm_gain, norm_shift):
    center = stream - jnp.mean(stream, -1, keepdims=True)
    spread = jnp.mean(center * center, -1, keepdims=True)
    return center * lax.rsqrt(spread + EPS_NORM) * norm_gain + norm_shift


def gelu_tanh(values):
    return (
        0.5
        * values
        * (1.0 + jnp.tanh(0.7978845608028654 * (values + 0.044715 * values * values * values)))
    )


def tokens_inner(left, right):
    return lax.dot_general(left, right, (((0,), (0,)), ((), ())), preferred_element_type=F32)


def against_rows(left, right):
    return lax.dot_general(left, right, (((1,), (1,)), ((), ())), preferred_element_type=F32)


def ring(values, axis, step):
    return lax.ppermute(values, RINGS[axis], [(i, (i + step) % 4) for i in range(4)])


def swap_cores(values):
    return lax.ppermute(values, "c", [(0, 1), (1, 0)])


def swap_halves(values):
    return lax.ppermute(values, ("c", "yl"), [(0, 0), (1, 2), (2, 1), (3, 3)])


def y_pairs(rule):
    pairs = []
    for y in range(4):
        for core in range(2):
            target = rule(y, core)
            if target is not None:
                y2, core2 = target[0] % 4, target[1]
                pairs.append(
                    ((y // 2) * 4 + core * 2 + y % 2, (y2 // 2) * 4 + core2 * 2 + y2 % 2)
                )
    return pairs


def fetch_weights(values, step):
    return lax.ppermute(
        values,
        ("yh", "c", "yl"),
        y_pairs(lambda y, c: (y - step, y % 2) if c == y % 2 else (y, y % 2)),
    )


def after(token, *values):
    return lax.optimization_barrier((token,) + values)[1:]


def run_beside(token, chain, tasks):
    results = [task(*after(token, *operands)) for task, operands in tasks]
    return lax.optimization_barrier((chain, results))


def gather_ring(values, tasks=()):
    before = ring(values, "z", 1)
    behind = ring(values, "z", -1)
    across = ring(values, "z", 2)
    return run_beside(values, jnp.concatenate([values, before, behind, across]), tasks)


def gather_pair(mine):
    return jnp.concatenate([mine, swap_cores(mine)])


def gather_rows(values, tasks=()):
    mine, results = gather_ring(values, tasks)
    return gather_pair(mine), results


def scatter_pair(left, product):
    half = left.shape[0] // 2
    other = swap_cores(product(left[half:]).astype(BF))
    return product(left[:half]) + other.astype(F32)


def scatter_rows(left, product, tasks=()):
    both = scatter_pair(left, product)
    low = both.astype(BF)
    rows = low.shape[0] // 4
    total = (
        both[:rows]
        + ring(low[rows : 2 * rows], "z", -1).astype(F32)
        + ring(low[2 * rows : 3 * rows], "z", 1).astype(F32)
        + ring(low[3 * rows :], "z", 2).astype(F32)
    )
    return run_beside(low, total, tasks)


def times(weight):
    return lambda left: jnp.dot(left, weight, preferred_element_type=F32)


def times_rows(weight):
    return lambda left: against_rows(left, weight)


def grad_blocks(pairs):
    place = lax.axis_index("x").astype(jnp.int32).reshape(1)
    tokens = pairs[0][0].shape[0]
    widths = [right.shape[1] for _, right in pairs]
    total = sum(widths)
    count = len(pairs)

    def kernel(place_ref, *refs):
        lefts, rights, outs = refs[: 2 * count], refs[2 * count : 3 * count], refs[3 * count :]
        step = pl.program_id(0)
        for d in range(4):

            @pl.when(step == d)
            def _():
                start = 0
                for i in range(count):
                    for high in range(2):
                        outs[d][high, :, start : start + widths[i]] = tokens_inner(
                            lefts[2 * i + high][...], rights[i][...]
                        ).astype(BF)
                    start += widths[i]

    def left_spec(high):
        return pl.BlockSpec((tokens, 128), lambda d, p: (0, high * 4 + lax.rem(p[0] + d, 4)))

    return pl.pallas_call(
        kernel,
        grid_spec=pltpu.PrefetchScalarGridSpec(
            num_scalar_prefetch=1,
            grid=(4,),
            in_specs=[left_spec(high) for _ in pairs for high in range(2)]
            + [pl.BlockSpec((tokens, width), lambda d, p: (0, 0)) for width in widths],
            out_specs=[pl.BlockSpec((2, 128, total), lambda d, p: (0, 0, 0))] * 4,
        ),
        out_shape=[jax.ShapeDtypeStruct((2, 128, total), BF)] * 4,
        compiler_params=pltpu.CompilerParams(vmem_limit_bytes=24 * 1024 * 1024),
        cost_estimate=pl.CostEstimate(
            flops=2 * tokens * 1024 * total, bytes_accessed=8 * 1024 * 1024, transcendentals=0
        ),
    )(place, *[left for left, _ in pairs for _ in range(2)], *[right for _, right in pairs])


def send_x(blocks):
    return blocks[0], ring(blocks[1], "x", 1), ring(blocks[3], "x", -1), ring(blocks[2], "x", 2)


def add_x(own, before, behind, across):
    summed = own.astype(F32) + before.astype(F32) + behind.astype(F32) + across.astype(F32)
    high, low_place = lax.axis_index("yh"), lax.axis_index("yl")
    y = high * 2 + low_place

    def pick(index):
        return jnp.where(index == 0, summed[0], summed[1])

    return (
        pick(high),
        pick(((y + 1) % 4) // 2).astype(BF),
        pick(((y + 3) % 4) // 2).astype(BF),
        pick(1 - high).astype(BF),
    )


def send_y(own, up, down, far):
    axes = ("yh", "c", "yl")
    return (
        own,
        lax.ppermute(up, axes, y_pairs(lambda y, c: (y + 1, c) if c != y % 2 else None)),
        lax.ppermute(down, axes, y_pairs(lambda y, c: (y + 3, c) if c != y % 2 else None)),
        lax.ppermute(far, axes, y_pairs(lambda y, c: (y + 2, c) if c == y % 2 else None)),
    )


def add_y(own, up, down, far):
    total = own + up.astype(F32) + down.astype(F32) + far.astype(F32)
    core = lax.axis_index("c")
    first, second = total[:64], total[64:]
    return jnp.where(core == 0, first, second), jnp.where(core == 0, second, first)


def send_core(keep, give):
    got = lax.ppermute(give, ("c", "yl"), [(0, 2), (3, 1)])
    return jnp.where(lax.axis_index("c") == lax.axis_index("yl"), keep, got)


def sum_everywhere(common, shard, steps, state):
    rows = common.shape[0]
    values = common
    for axis, step in zip(("z", "x", "y"), steps):
        if axis == "x":
            values = jnp.concatenate([values, shard])
        values = (values + ring(values, axis, 2)) + (
            ring(values, axis, 1) + ring(values, axis, -1)
        )
        values, state = lax.optimization_barrier((values, state))
        state = step(*state)
    other = swap_cores(values)
    own = lax.axis_index("c") == lax.axis_index("yl")
    return values[:rows] + other[:rows], jnp.where(own, values[rows:], other[rows:]), state


def block_slots():
    core, z = lax.axis_index("c"), lax.axis_index("z")
    blocks = lax.iota(jnp.int32, 8)
    turn = (blocks % 4 - z + 4) % 4
    order = jnp.where(turn == 0, 0, jnp.where(turn == 3, 1, turn + 1))
    return (jnp.where(blocks // 4 == core, 0, 4) + order).astype(jnp.int32)


BLOCK = 128
QUERY_ROWS = 256
VMEM_BYTES = 32 * 1024 * 1024


def slot_rows(slots, block):
    return pl.ds(pl.multiple_of(slots[block] * BLOCK, BLOCK), BLOCK)


def masked_scores(keys, queries):
    scores = against_rows(keys, queries)
    count = queries.shape[0]
    shape = (count, count)
    mask = lax.broadcasted_iota(jnp.int32, shape, 1) >= lax.broadcasted_iota(jnp.int32, shape, 0)
    diagonal = jnp.where(mask, scores[-count:], NEG_FILL)
    if keys.shape[0] == count:
        return diagonal
    return jnp.concatenate([scores[:-count], diagonal])


def attend_forward_kernel(slots, low_ref, high_ref, k_ref, v_ref, out_ref, log_ref, k_all, v_all):
    step = pl.program_id(0)

    @pl.when(step == 0)
    def _():
        for block in range(8):
            k_all[block * BLOCK : (block + 1) * BLOCK, :] = k_ref[slot_rows(slots, block), :]
            v_all[block * BLOCK : (block + 1) * BLOCK, :] = v_ref[slot_rows(slots, block), :]

    for part in range(k_ref.shape[0] // QUERY_ROWS):

        @pl.when(step == part)
        def _():
            end = (part + 1) * QUERY_ROWS
            queries = jnp.concatenate([low_ref[...], high_ref[...]]) * HEAD_DIM ** (-0.5)
            for head in range(k_ref.shape[1] // HEAD_DIM):
                cut = slice(head * HEAD_DIM, (head + 1) * HEAD_DIM)
                scores = masked_scores(k_all[:end, cut], queries[:, cut])
                peak = jnp.max(scores, 0, keepdims=True)
                weights = jnp.exp(scores - peak)
                total = jnp.sum(weights, 0, keepdims=True)
                weights = (weights * (1.0 / total)).astype(BF)
                mixed = tokens_inner(v_all[:end, cut], weights).T.astype(BF)
                out_ref[slot_rows(slots, 2 * part), cut] = mixed[:BLOCK]
                out_ref[slot_rows(slots, 2 * part + 1), cut] = mixed[BLOCK:]
                log_ref[head : head + 1, :] = peak + jnp.log(total)


def query_specs(width):
    return [
        pl.BlockSpec((BLOCK, width), lambda i, s: (s[2 * i], 0)),
        pl.BlockSpec((BLOCK, width), lambda i, s: (s[2 * i + 1], 0)),
    ]


def attend_forward(qkv, slots):
    tokens, width = qkv.shape[0], qkv.shape[1] // 3
    heads = width // HEAD_DIM
    return pl.pallas_call(
        attend_forward_kernel,
        grid_spec=pltpu.PrefetchScalarGridSpec(
            num_scalar_prefetch=1,
            grid=(tokens // QUERY_ROWS,),
            in_specs=query_specs(width)
            + [
                pl.BlockSpec((tokens, width), lambda i, s: (0, 1)),
                pl.BlockSpec((tokens, width), lambda i, s: (0, 2)),
            ],
            out_specs=[
                pl.BlockSpec((tokens, width), lambda i, s: (0, 0)),
                pl.BlockSpec((heads, QUERY_ROWS), lambda i, s: (0, i)),
            ],
            scratch_shapes=[pltpu.VMEM((tokens, width), BF), pltpu.VMEM((tokens, width), BF)],
        ),
        out_shape=[
            jax.ShapeDtypeStruct((tokens, width), BF),
            jax.ShapeDtypeStruct((heads, tokens), F32),
        ],
        compiler_params=pltpu.CompilerParams(vmem_limit_bytes=VMEM_BYTES),
        cost_estimate=pl.CostEstimate(
            flops=8 * tokens * tokens * width,
            bytes_accessed=2 ** 21,
            transcendentals=tokens * tokens * heads,
        ),
    )(slots, qkv, qkv, qkv, qkv)


def attend_backward_kernel(
    slots, log_ref, low_ref, high_ref, k_ref, v_ref, do_low, do_high, out_ref,
    k_all, v_all, dk_ref, dv_ref,
):
    step = pl.program_id(0)
    width = k_ref.shape[1]
    scale = HEAD_DIM ** (-0.5)

    @pl.when(step == 0)
    def _():
        dk_ref[...] = jnp.zeros_like(dk_ref)
        dv_ref[...] = jnp.zeros_like(dv_ref)
        for block in range(8):
            k_all[block * BLOCK : (block + 1) * BLOCK, :] = k_ref[slot_rows(slots, block), :]
            v_all[block * BLOCK : (block + 1) * BLOCK, :] = v_ref[slot_rows(slots, block), :]

    for part in range(k_ref.shape[0] // QUERY_ROWS):

        @pl.when(step == part)
        def _():
            end = (part + 1) * QUERY_ROWS
            queries = jnp.concatenate([low_ref[...], high_ref[...]]) * scale
            grad_out = jnp.concatenate([do_low[...], do_high[...]])
            for head in range(width // HEAD_DIM):
                cut = slice(head * HEAD_DIM, (head + 1) * HEAD_DIM)
                q, k, v, do = queries[:, cut], k_all[:end, cut], v_all[:end, cut], grad_out[:, cut]
                weights = jnp.exp(masked_scores(k, q) - log_ref[head : head + 1, :])
                grad_weights = against_rows(v, do)
                mean = jnp.sum(weights * grad_weights, 0, keepdims=True)
                grad_scores = (weights * (grad_weights - mean)).astype(BF)
                dq = (tokens_inner(k, grad_scores).T * scale).astype(BF)
                out_ref[slot_rows(slots, 2 * part), cut] = dq[:BLOCK]
                out_ref[slot_rows(slots, 2 * part + 1), cut] = dq[BLOCK:]
                dk_ref[:end, cut] += jnp.dot(grad_scores, q, preferred_element_type=F32)
                dv_ref[:end, cut] += jnp.dot(weights.astype(BF), do, preferred_element_type=F32)

    @pl.when(step == pl.num_programs(0) - 1)
    def _():
        for block in range(8):
            rows = slice(block * BLOCK, (block + 1) * BLOCK)
            out_ref[slot_rows(slots, block), width : 2 * width] = dk_ref[rows, :].astype(BF)
            out_ref[slot_rows(slots, block), 2 * width :] = dv_ref[rows, :].astype(BF)


def attend_backward(qkv, grad_out, log_totals, slots):
    tokens, width = qkv.shape[0], qkv.shape[1] // 3
    heads = width // HEAD_DIM
    return pl.pallas_call(
        attend_backward_kernel,
        grid_spec=pltpu.PrefetchScalarGridSpec(
            num_scalar_prefetch=1,
            grid=(tokens // QUERY_ROWS,),
            in_specs=[pl.BlockSpec((heads, QUERY_ROWS), lambda i, s: (0, i))]
            + query_specs(width)
            + [
                pl.BlockSpec((tokens, width), lambda i, s: (0, 1)),
                pl.BlockSpec((tokens, width), lambda i, s: (0, 2)),
            ]
            + query_specs(width),
            out_specs=pl.BlockSpec((tokens, 3 * width), lambda i, s: (0, 0)),
            scratch_shapes=[
                pltpu.VMEM((tokens, width), BF),
                pltpu.VMEM((tokens, width), BF),
                pltpu.VMEM((tokens, width), F32),
                pltpu.VMEM((tokens, width), F32),
            ],
        ),
        out_shape=jax.ShapeDtypeStruct((tokens, 3 * width), BF),
        compiler_params=pltpu.CompilerParams(vmem_limit_bytes=VMEM_BYTES),
        cost_estimate=pl.CostEstimate(
            flops=20 * tokens * tokens * width,
            bytes_accessed=2 ** 22,
            transcendentals=tokens * tokens * heads,
        ),
    )(slots, log_totals, qkv, qkv, qkv, qkv, grad_out, grad_out)


def per_device(
    hidden_in,
    cotangent,
    norm_gain,
    norm_shift,
    inward,
    inward_bias,
    outward,
    outward_bias,
    expand,
    expand_bias,
    shrink,
    shrink_bias,
):
    stream = swap_halves(hidden_in).astype(F32)
    columns = inward.shape[3]
    w_in, w_out, w_up, w_down = [], [], [], []
    for layer in range(LAYERS):
        w_in.append(fetch_weights(inward[layer].reshape(-1, 3 * columns), 1))
        if layer == 0:
            biases = fetch_weights(
                jnp.concatenate([inward_bias.reshape(-1, 128), expand_bias.reshape(-1, 128)]), -1
            )
            bias_in = biases[:4].reshape(LAYERS, 2, columns)
            bias_up = biases[4:].reshape(LAYERS, -1)
        w_out.append(fetch_weights(outward[layer], -1))
        w_up.append(fetch_weights(expand[layer], -1))
        w_down.append(fetch_weights(shrink[layer], 1))
    cotangent = swap_halves(cotangent)

    slots = block_slots()
    saved = []
    pieces = {}

    def cotangent_task(step):
        def task(values):
            pieces[step] = ring(values, "z", step)
            return pieces[step]

        return [(task, (cotangent,))]

    for layer in range(LAYERS):
        normed = layer_norm(stream, norm_gain[layer, 0], norm_shift[layer, 0]).astype(BF)
        mine, _ = gather_ring(normed)
        if layer == 1:
            mine, w_up[1], w_down[1] = lax.optimization_barrier((mine, w_up[1], w_down[1]))
        normed_all = gather_pair(mine)
        if layer == 0:
            normed_all, w_up[0] = lax.optimization_barrier((normed_all, w_up[0]))
        qkv_bias = jnp.concatenate(
            [bias_in[layer, 0], jnp.zeros((columns,), F32), bias_in[layer, 1]]
        )
        qkv = (
            jnp.dot(normed_all, w_in[layer], preferred_element_type=F32) + qkv_bias
        ).astype(BF)
        attended, log_totals = attend_forward(qkv, slots)
        attended, (piece,) = run_beside(
            normed_all, attended, cotangent_task(1 if layer == 0 else 2)
        )
        pieces[1 if layer == 0 else 2] = piece
        if layer == 0:
            attended, w_down[0] = lax.optimization_barrier((attended, w_down[0]))
        middle = stream + (
            scatter_rows(attended, times(w_out[layer]))[0]
            + outward_bias[layer]
        )
        normed_mid = layer_norm(middle, norm_gain[layer, 1], norm_shift[layer, 1]).astype(BF)
        mid_mine, _ = gather_ring(normed_mid)
        if layer == 0:
            mid_mine, w_in[1], w_out[1] = lax.optimization_barrier((mid_mine, w_in[1], w_out[1]))
        mid_all = gather_pair(mid_mine)
        hidden_pre = (
            jnp.dot(mid_all, w_up[layer], preferred_element_type=F32) + bias_up[layer]
        )
        activated = gelu_tanh(hidden_pre).astype(BF)
        saved.append(
            (stream, normed_all, qkv, attended, log_totals, middle, mid_all, hidden_pre,
             activated)
        )
        if layer == 0:
            activated, (pieces[-1],) = run_beside(mid_mine, activated, cotangent_task(-1))
            stream = middle + (
                scatter_rows(activated, times(w_down[layer]))[0]
                + shrink_bias[layer]
            )
    cotangent_ring = jnp.concatenate([cotangent, pieces[1], pieces[-1], pieces[2]])

    grad_stream = cotangent.astype(F32)
    gains, shifts, sums_out, sums_down, sums_in, sums_up = {}, {}, {}, {}, {}, {}
    grads_mlp, grads_attn = [None] * LAYERS, [None] * LAYERS

    _, normed_all, qkv, attended, log_totals, middle, mid_all, hidden_pre, activated = saved[1]
    sums_down[1] = jnp.sum(cotangent, 0, dtype=F32)
    dy_all = gather_pair(cotangent_ring)

    def mlp_back(layer, dy_all):
        hidden_pre = saved[layer][7]
        grad_act = against_rows(dy_all, w_down[layer])
        du = jax.vjp(gelu_tanh, hidden_pre)[1](grad_act)[0].astype(BF)
        return du

    def mlp_sum(layer, du, dy_all, tasks):
        _, _, _, _, _, middle, mid_all, hidden_pre, activated = saved[layer]
        sums_up[layer] = jnp.sum(du, 0, dtype=F32)

        def make(dy_all, activated, mid_all, du):
            return grad_blocks([(dy_all, activated), (mid_all, du)])

        dh, results = scatter_rows(
            du, times_rows(w_up[layer]), [(make, (dy_all, activated, mid_all, du))] + tasks
        )
        back_mid = jax.vjp(layer_norm, middle, norm_gain[layer, 1], norm_shift[layer, 1])[1]
        grad_part, gains[layer, 1], shifts[layer, 1] = back_mid(dh)
        return grad_part, results

    def attn_sum(layer, dqkv, dz_all, tasks):
        stream, normed_all, _, attended, _, _, _, _, _ = saved[layer]
        sums = jnp.sum(dqkv, 0, dtype=F32)
        sums_in[layer] = jnp.stack([sums[:columns], sums[2 * columns :]])

        def make(dz_all, attended, normed_all, dqkv):
            return grad_blocks([(dz_all, attended), (normed_all, dqkv)])

        da, results = scatter_rows(
            dqkv, times_rows(w_in[layer]), [(make, (dz_all, attended, normed_all, dqkv))] + tasks
        )
        back_in = jax.vjp(layer_norm, stream, norm_gain[layer, 0], norm_shift[layer, 0])[1]
        grad_first, gains[layer, 0], shifts[layer, 0] = back_in(da)
        return grad_first, results

    du = mlp_back(1, dy_all)
    grad_part, (mlp1,) = mlp_sum(1, du, dy_all, [])
    grad_middle = grad_stream + grad_part
    mlp1 = send_x(mlp1)
    dz = grad_middle.astype(BF)
    sums_out[1] = jnp.sum(dz, 0, dtype=F32)
    dz_mine, _ = gather_ring(dz)
    dz_mine, near1 = lax.optimization_barrier((dz_mine, mlp1[:3]))
    dz_all = gather_pair(dz_mine)
    do = against_rows(dz_all, w_out[1]).astype(BF)
    dqkv = attend_backward(qkv, do, log_totals, slots)

    def last_pairs(activated):
        both = scatter_pair(activated, times(w_down[1]))
        low = both.astype(BF)
        rows = low.shape[0] // 4
        near = (
            both[:rows]
            + ring(low[rows : 2 * rows], "z", -1).astype(F32)
            + ring(low[2 * rows : 3 * rows], "z", 1).astype(F32)
        )
        return near, low[3 * rows :]

    dqkv, ((last_near, last_far),) = run_beside(dz_all, dqkv, [(last_pairs, (activated,))])
    dqkv, mlp1 = lax.optimization_barrier((dqkv, (*near1, mlp1[3])))
    mlp1 = send_y(*add_x(*mlp1))
    grad_first, (attn1, mlp1) = attn_sum(1, dqkv, dz_all, [(add_y, mlp1)])
    grad_stream = grad_middle + grad_first
    attn1 = send_x(attn1)
    grads_mlp[1] = send_core(*mlp1)

    _, normed_all, qkv, attended, log_totals, middle, mid_all, hidden_pre, activated = saved[0]
    dy = grad_stream.astype(BF)
    sums_down[0] = jnp.sum(dy, 0, dtype=F32)
    dy_mine, _ = gather_ring(dy)
    dy_mine, attn1 = lax.optimization_barrier((dy_mine, attn1))
    attn1 = send_y(*add_x(*attn1))
    dy_all = gather_pair(dy_mine)
    du = mlp_back(0, dy_all)
    du, (last_across,) = run_beside(
        dy_mine, du, [(lambda values: ring(values, "z", 2), (last_far,))]
    )
    hidden_out = saved[1][5] + (last_near + last_across.astype(F32) + shrink_bias[1])
    hidden_out = swap_halves(hidden_out.astype(BF)).astype(F32)
    du, attn1 = lax.optimization_barrier((du, attn1))
    grad_part, (mlp0, attn1) = mlp_sum(0, du, dy_all, [(add_y, attn1)])
    grad_middle = grad_stream + grad_part
    mlp0 = send_x(mlp0)
    grads_attn[1] = send_core(*attn1)
    dz = grad_middle.astype(BF)
    sums_out[0] = jnp.sum(dz, 0, dtype=F32)
    dz_mine, _ = gather_ring(dz)
    dz_mine, near0 = lax.optimization_barrier((dz_mine, mlp0[:3]))
    dz_all = gather_pair(dz_mine)
    do = against_rows(dz_all, w_out[0]).astype(BF)
    dqkv = attend_backward(qkv, do, log_totals, slots)
    dqkv, mlp0 = lax.optimization_barrier((dqkv, (*near0, mlp0[3])))
    mlp0 = send_y(*add_x(*mlp0))
    grad_first, (attn0, mlp0) = attn_sum(0, dqkv, dz_all, [(add_y, mlp0)])
    grad_stream = grad_middle + grad_first
    grad_hidden = swap_halves(grad_stream.astype(BF)).astype(F32)
    grads_mlp[0] = send_core(*mlp0)

    both = range(LAYERS)
    common = jnp.concatenate(
        [
            m.reshape(-1, 128)
            for m in (
                [gains[n, i] for n in both for i in (0, 1)]
                + [shifts[n, i] for n in both for i in (0, 1)]
                + [sums_out[n] for n in both]
                + [sums_down[n] for n in both]
            )
        ]
    )
    shard = jnp.concatenate(
        [m.reshape(-1, 128) for m in [sums_up[n] for n in both] + [sums_in[n] for n in both]]
    )
    common, shard, grads_attn[0] = sum_everywhere(
        common,
        shard,
        (
            lambda *m: m,
            lambda *m: send_y(*add_x(*m)),
            lambda *m: send_core(*add_y(*m)),
        ),
        send_x(attn0),
    )
    grad_gain = common[:32].reshape(LAYERS, 2, 1024)
    grad_shift = common[32:64].reshape(LAYERS, 2, 1024)
    grad_out_bias = common[64:80].reshape(LAYERS, 1024)
    grad_down_bias = common[80:96].reshape(LAYERS, 1024)
    grad_up_bias = shard[:8].reshape(LAYERS, -1)
    grad_in_bias = shard[8:].reshape(LAYERS, 2, columns)

    width = shrink.shape[1]
    return (
        hidden_out,
        grad_hidden,
        grad_gain,
        grad_shift,
        jnp.stack([g[:, columns:].reshape(-1, 3, columns) for g in grads_attn]),
        grad_in_bias,
        jnp.stack([g[:, :columns].T for g in grads_attn]),
        grad_out_bias,
        jnp.stack([g[:, width:] for g in grads_mlp]),
        grad_up_bias,
        jnp.stack([g[:, :width].T for g in grads_mlp]),
        grad_down_bias,
    )


def solution(mesh):
    fine = Mesh(mesh.devices.reshape(2, 4, 2, 2, 4), ("yh", "x", "c", "yl", "z"))
    dp, tensor = ("yh", "x", "c"), ("yl", "z")
    rows = P(dp + tensor, None)
    return jax.shard_map(
        per_device,
        mesh=fine,
        in_specs=(
            rows,
            rows,
            P(),
            P(),
            P(None, None, None, tensor),
            P(None, None, tensor),
            P(None, tensor, None),
            P(),
            P(None, None, tensor),
            P(None, tensor),
            P(None, tensor, None),
            P(),
        ),
        out_specs=(
            rows,
            rows,
            P(),
            P(),
            P(None, dp, None, tensor),
            P(None, None, tensor),
            P(None, tensor, dp),
            P(),
            P(None, dp, tensor),
            P(None, tensor),
            P(None, tensor, dp),
            P(),
        ),
        check_vma=False,
    )
```

```python
import jax
import jax.numpy as jnp
from jax import lax
from jax.experimental import pallas as pl
from jax.experimental.pallas import tpu as pltpu
from jax.sharding import Mesh
from jax.sharding import PartitionSpec as P

HEAD_DIM = 64
LAYERS = 2
EPS_NORM = 1e-05
NEG_FILL = -1000000000.0
BF = jnp.bfloat16
F32 = jnp.float32
RINGS = {"z": ("z",), "x": ("x",), "y": ("yh", "yl")}


def layer_norm(stream, norm_gain, norm_shift):
    center = stream - jnp.mean(stream, -1, keepdims=True)
    spread = jnp.mean(center * center, -1, keepdims=True)
    return center * lax.rsqrt(spread + EPS_NORM) * norm_gain + norm_shift


def gelu_tanh(values):
    return (
        0.5
        * values
        * (1.0 + jnp.tanh(0.7978845608028654 * (values + 0.044715 * values * values * values)))
    )


def tokens_inner(left, right):
    return lax.dot_general(left, right, (((0,), (0,)), ((), ())), preferred_element_type=F32)


def against_rows(left, right):
    return lax.dot_general(left, right, (((1,), (1,)), ((), ())), preferred_element_type=F32)


def ring(values, axis, step):
    return lax.ppermute(values, RINGS[axis], [(i, (i + step) % 4) for i in range(4)])


def swap_cores(values):
    return lax.ppermute(values, "c", [(0, 1), (1, 0)])


def swap_halves(values):
    return lax.ppermute(values, ("c", "yl"), [(0, 0), (1, 2), (2, 1), (3, 3)])


def y_pairs(rule):
    pairs = []
    for y in range(4):
        for core in range(2):
            target = rule(y, core)
            if target is not None:
                y2, core2 = target[0] % 4, target[1]
                pairs.append(
                    ((y // 2) * 4 + core * 2 + y % 2, (y2 // 2) * 4 + core2 * 2 + y2 % 2)
                )
    return pairs


def fetch_weights(values, step):
    return lax.ppermute(
        values,
        ("yh", "c", "yl"),
        y_pairs(lambda y, c: (y - step, y % 2) if c == y % 2 else (y, y % 2)),
    )


def after(token, *values):
    return lax.optimization_barrier((token,) + values)[1:]


def run_beside(token, chain, tasks):
    results = [task(*after(token, *operands)) for task, operands in tasks]
    return lax.optimization_barrier((chain, results))


def gather_ring(values, tasks=()):
    before = ring(values, "z", 1)
    behind = ring(values, "z", -1)
    across = ring(values, "z", 2)
    return run_beside(values, jnp.concatenate([values, before, behind, across]), tasks)


def gather_pair(mine):
    return jnp.concatenate([mine, swap_cores(mine)])


def gather_rows(values, tasks=()):
    mine, results = gather_ring(values, tasks)
    return gather_pair(mine), results


def scatter_pair(left, product):
    half = left.shape[0] // 2
    other = swap_cores(product(left[half:]).astype(BF))
    return product(left[:half]) + other.astype(F32)


def scatter_rows(left, product, tasks=()):
    both = scatter_pair(left, product)
    low = both.astype(BF)
    rows = low.shape[0] // 4
    total = (
        both[:rows]
        + ring(low[rows : 2 * rows], "z", -1).astype(F32)
        + ring(low[2 * rows : 3 * rows], "z", 1).astype(F32)
        + ring(low[3 * rows :], "z", 2).astype(F32)
    )
    return run_beside(low, total, tasks)


def times(weight):
    return lambda left: jnp.dot(left, weight, preferred_element_type=F32)


def times_rows(weight):
    return lambda left: against_rows(left, weight)


def grad_blocks(pairs):
    place = lax.axis_index("x").astype(jnp.int32).reshape(1)
    tokens = pairs[0][0].shape[0]
    widths = [right.shape[1] for _, right in pairs]
    total = sum(widths)
    count = len(pairs)

    def kernel(place_ref, *refs):
        lefts, rights, outs = refs[: 2 * count], refs[2 * count : 3 * count], refs[3 * count :]
        step = pl.program_id(0)
        for d in range(4):

            @pl.when(step == d)
            def _():
                start = 0
                for i in range(count):
                    for high in range(2):
                        outs[d][high, :, start : start + widths[i]] = tokens_inner(
                            lefts[2 * i + high][...], rights[i][...]
                        ).astype(BF)
                    start += widths[i]

    def left_spec(high):
        return pl.BlockSpec((tokens, 128), lambda d, p: (0, high * 4 + lax.rem(p[0] + d, 4)))

    return pl.pallas_call(
        kernel,
        grid_spec=pltpu.PrefetchScalarGridSpec(
            num_scalar_prefetch=1,
            grid=(4,),
            in_specs=[left_spec(high) for _ in pairs for high in range(2)]
            + [pl.BlockSpec((tokens, width), lambda d, p: (0, 0)) for width in widths],
            out_specs=[pl.BlockSpec((2, 128, total), lambda d, p: (0, 0, 0))] * 4,
        ),
        out_shape=[jax.ShapeDtypeStruct((2, 128, total), BF)] * 4,
        compiler_params=pltpu.CompilerParams(vmem_limit_bytes=24 * 1024 * 1024),
        cost_estimate=pl.CostEstimate(
            flops=2 * tokens * 1024 * total, bytes_accessed=8 * 1024 * 1024, transcendentals=0
        ),
    )(place, *[left for left, _ in pairs for _ in range(2)], *[right for _, right in pairs])


def send_x(blocks):
    return blocks[0], ring(blocks[1], "x", 1), ring(blocks[3], "x", -1), ring(blocks[2], "x", 2)


def add_x(own, before, behind, across):
    summed = own.astype(F32) + before.astype(F32) + behind.astype(F32) + across.astype(F32)
    high, low_place = lax.axis_index("yh"), lax.axis_index("yl")
    y = high * 2 + low_place

    def pick(index):
        return jnp.where(index == 0, summed[0], summed[1])

    return (
        pick(high),
        pick(((y + 1) % 4) // 2).astype(BF),
        pick(((y + 3) % 4) // 2).astype(BF),
        pick(1 - high).astype(BF),
    )


def send_y(own, up, down, far):
    axes = ("yh", "c", "yl")
    return (
        own,
        lax.ppermute(up, axes, y_pairs(lambda y, c: (y + 1, c) if c != y % 2 else None)),
        lax.ppermute(down, axes, y_pairs(lambda y, c: (y + 3, c) if c != y % 2 else None)),
        lax.ppermute(far, axes, y_pairs(lambda y, c: (y + 2, c) if c == y % 2 else None)),
    )


def add_y(own, up, down, far):
    total = own + up.astype(F32) + down.astype(F32) + far.astype(F32)
    core = lax.axis_index("c")
    first, second = total[:64], total[64:]
    return jnp.where(core == 0, first, second), jnp.where(core == 0, second, first)


def send_core(keep, give):
    got = lax.ppermute(give, ("c", "yl"), [(0, 2), (3, 1)])
    return jnp.where(lax.axis_index("c") == lax.axis_index("yl"), keep, got)


def sum_everywhere(common, shard, steps, state):
    rows = common.shape[0]
    values = common
    for axis, step in zip(("z", "x", "y"), steps):
        if axis == "x":
            values = jnp.concatenate([values, shard])
        values = (values + ring(values, axis, 2)) + (
            ring(values, axis, 1) + ring(values, axis, -1)
        )
        values, state = lax.optimization_barrier((values, state))
        state = step(*state)
    other = swap_cores(values)
    own = lax.axis_index("c") == lax.axis_index("yl")
    return values[:rows] + other[:rows], jnp.where(own, values[rows:], other[rows:]), state


def block_slots():
    core, z = lax.axis_index("c"), lax.axis_index("z")
    blocks = lax.iota(jnp.int32, 8)
    turn = (blocks % 4 - z + 4) % 4
    order = jnp.where(turn == 0, 0, jnp.where(turn == 3, 1, turn + 1))
    return (jnp.where(blocks // 4 == core, 0, 4) + order).astype(jnp.int32)


BLOCK = 128
QUERY_ROWS = 256
VMEM_BYTES = 32 * 1024 * 1024


def slot_rows(slots, block):
    return pl.ds(pl.multiple_of(slots[block] * BLOCK, BLOCK), BLOCK)


def masked_scores(keys, queries):
    scores = against_rows(keys, queries)
    count = queries.shape[0]
    shape = (count, count)
    mask = lax.broadcasted_iota(jnp.int32, shape, 1) >= lax.broadcasted_iota(jnp.int32, shape, 0)
    diagonal = jnp.where(mask, scores[-count:], NEG_FILL)
    if keys.shape[0] == count:
        return diagonal
    return jnp.concatenate([scores[:-count], diagonal])


def attend_forward_kernel(slots, low_ref, high_ref, k_ref, v_ref, out_ref, log_ref, k_all, v_all):
    step = pl.program_id(0)

    @pl.when(step == 0)
    def _():
        for block in range(8):
            k_all[block * BLOCK : (block + 1) * BLOCK, :] = k_ref[slot_rows(slots, block), :]
            v_all[block * BLOCK : (block + 1) * BLOCK, :] = v_ref[slot_rows(slots, block), :]

    for part in range(k_ref.shape[0] // QUERY_ROWS):

        @pl.when(step == part)
        def _():
            end = (part + 1) * QUERY_ROWS
            queries = jnp.concatenate([low_ref[...], high_ref[...]]) * HEAD_DIM ** (-0.5)
            for head in range(k_ref.shape[1] // HEAD_DIM):
                cut = slice(head * HEAD_DIM, (head + 1) * HEAD_DIM)
                scores = masked_scores(k_all[:end, cut], queries[:, cut])
                peak = jnp.max(scores, 0, keepdims=True)
                weights = jnp.exp(scores - peak)
                total = jnp.sum(weights, 0, keepdims=True)
                weights = (weights * (1.0 / total)).astype(BF)
                mixed = tokens_inner(v_all[:end, cut], weights).T.astype(BF)
                out_ref[slot_rows(slots, 2 * part), cut] = mixed[:BLOCK]
                out_ref[slot_rows(slots, 2 * part + 1), cut] = mixed[BLOCK:]
                log_ref[head : head + 1, :] = peak + jnp.log(total)


def query_specs(width):
    return [
        pl.BlockSpec((BLOCK, width), lambda i, s: (s[2 * i], 0)),
        pl.BlockSpec((BLOCK, width), lambda i, s: (s[2 * i + 1], 0)),
    ]


def attend_forward(qkv, slots):
    tokens, width = qkv.shape[0], qkv.shape[1] // 3
    heads = width // HEAD_DIM
    return pl.pallas_call(
        attend_forward_kernel,
        grid_spec=pltpu.PrefetchScalarGridSpec(
            num_scalar_prefetch=1,
            grid=(tokens // QUERY_ROWS,),
            in_specs=query_specs(width)
            + [
                pl.BlockSpec((tokens, width), lambda i, s: (0, 1)),
                pl.BlockSpec((tokens, width), lambda i, s: (0, 2)),
            ],
            out_specs=[
                pl.BlockSpec((tokens, width), lambda i, s: (0, 0)),
                pl.BlockSpec((heads, QUERY_ROWS), lambda i, s: (0, i)),
            ],
            scratch_shapes=[pltpu.VMEM((tokens, width), BF), pltpu.VMEM((tokens, width), BF)],
        ),
        out_shape=[
            jax.ShapeDtypeStruct((tokens, width), BF),
            jax.ShapeDtypeStruct((heads, tokens), F32),
        ],
        compiler_params=pltpu.CompilerParams(vmem_limit_bytes=VMEM_BYTES),
        cost_estimate=pl.CostEstimate(
            flops=8 * tokens * tokens * width,
            bytes_accessed=2 ** 21,
            transcendentals=tokens * tokens * heads,
        ),
    )(slots, qkv, qkv, qkv, qkv)


def attend_backward_kernel(
    slots, log_ref, low_ref, high_ref, k_ref, v_ref, do_low, do_high, out_ref,
    k_all, v_all, dk_ref, dv_ref,
):
    step = pl.program_id(0)
    width = k_ref.shape[1]
    scale = HEAD_DIM ** (-0.5)

    @pl.when(step == 0)
    def _():
        dk_ref[...] = jnp.zeros_like(dk_ref)
        dv_ref[...] = jnp.zeros_like(dv_ref)
        for block in range(8):
            k_all[block * BLOCK : (block + 1) * BLOCK, :] = k_ref[slot_rows(slots, block), :]
            v_all[block * BLOCK : (block + 1) * BLOCK, :] = v_ref[slot_rows(slots, block), :]

    for part in range(k_ref.shape[0] // QUERY_ROWS):

        @pl.when(step == part)
        def _():
            end = (part + 1) * QUERY_ROWS
            queries = jnp.concatenate([low_ref[...], high_ref[...]]) * scale
            grad_out = jnp.concatenate([do_low[...], do_high[...]])
            for head in range(width // HEAD_DIM):
                cut = slice(head * HEAD_DIM, (head + 1) * HEAD_DIM)
                q, k, v, do = queries[:, cut], k_all[:end, cut], v_all[:end, cut], grad_out[:, cut]
                weights = jnp.exp(masked_scores(k, q) - log_ref[head : head + 1, :])
                grad_weights = against_rows(v, do)
                mean = jnp.sum(weights * grad_weights, 0, keepdims=True)
                grad_scores = (weights * (grad_weights - mean)).astype(BF)
                dq = (tokens_inner(k, grad_scores).T * scale).astype(BF)
                out_ref[slot_rows(slots, 2 * part), cut] = dq[:BLOCK]
                out_ref[slot_rows(slots, 2 * part + 1), cut] = dq[BLOCK:]
                dk_ref[:end, cut] += jnp.dot(grad_scores, q, preferred_element_type=F32)
                dv_ref[:end, cut] += jnp.dot(weights.astype(BF), do, preferred_element_type=F32)

    @pl.when(step == pl.num_programs(0) - 1)
    def _():
        for block in range(8):
            rows = slice(block * BLOCK, (block + 1) * BLOCK)
            out_ref[slot_rows(slots, block), width : 2 * width] = dk_ref[rows, :].astype(BF)
            out_ref[slot_rows(slots, block), 2 * width :] = dv_ref[rows, :].astype(BF)


def attend_backward(qkv, grad_out, log_totals, slots):
    tokens, width = qkv.shape[0], qkv.shape[1] // 3
    heads = width // HEAD_DIM
    return pl.pallas_call(
        attend_backward_kernel,
        grid_spec=pltpu.PrefetchScalarGridSpec(
            num_scalar_prefetch=1,
            grid=(tokens // QUERY_ROWS,),
            in_specs=[pl.BlockSpec((heads, QUERY_ROWS), lambda i, s: (0, i))]
            + query_specs(width)
            + [
                pl.BlockSpec((tokens, width), lambda i, s: (0, 1)),
                pl.BlockSpec((tokens, width), lambda i, s: (0, 2)),
            ]
            + query_specs(width),
            out_specs=pl.BlockSpec((tokens, 3 * width), lambda i, s: (0, 0)),
            scratch_shapes=[
                pltpu.VMEM((tokens, width), BF),
                pltpu.VMEM((tokens, width), BF),
                pltpu.VMEM((tokens, width), F32),
                pltpu.VMEM((tokens, width), F32),
            ],
        ),
        out_shape=jax.ShapeDtypeStruct((tokens, 3 * width), BF),
        compiler_params=pltpu.CompilerParams(vmem_limit_bytes=VMEM_BYTES),
        cost_estimate=pl.CostEstimate(
            flops=20 * tokens * tokens * width,
            bytes_accessed=2 ** 22,
            transcendentals=tokens * tokens * heads,
        ),
    )(slots, log_totals, qkv, qkv, qkv, qkv, grad_out, grad_out)


def per_device(
    hidden_in,
    cotangent,
    norm_gain,
    norm_shift,
    inward,
    inward_bias,
    outward,
    outward_bias,
    expand,
    expand_bias,
    shrink,
    shrink_bias,
):
    stream = swap_halves(hidden_in).astype(F32)
    columns = inward.shape[3]
    w_in, w_out, w_up, w_down = [], [], [], []
    for layer in range(LAYERS):
        w_in.append(fetch_weights(inward[layer].reshape(-1, 3 * columns), 1))
        if layer == 0:
            biases = fetch_weights(
                jnp.concatenate([inward_bias.reshape(-1, 128), expand_bias.reshape(-1, 128)]), -1
            )
            bias_in = biases[:4].reshape(LAYERS, 2, columns)
            bias_up = biases[4:].reshape(LAYERS, -1)
        w_out.append(fetch_weights(outward[layer], -1))
        w_up.append(fetch_weights(expand[layer], -1))
        w_down.append(fetch_weights(shrink[layer], 1))
    cotangent = swap_halves(cotangent)

    slots = block_slots()
    saved = []
    pieces = {}

    def cotangent_task(step):
        def task(values):
            pieces[step] = ring(values, "z", step)
            return pieces[step]

        return [(task, (cotangent,))]

    for layer in range(LAYERS):
        normed = layer_norm(stream, norm_gain[layer, 0], norm_shift[layer, 0]).astype(BF)
        mine, _ = gather_ring(normed)
        if layer == 1:
            mine, w_up[1], w_down[1] = lax.optimization_barrier((mine, w_up[1], w_down[1]))
        normed_all = gather_pair(mine)
        if layer == 0:
            normed_all, w_up[0] = lax.optimization_barrier((normed_all, w_up[0]))
        qkv_bias = jnp.concatenate(
            [bias_in[layer, 0], jnp.zeros((columns,), F32), bias_in[layer, 1]]
        )
        qkv = (
            jnp.dot(normed_all, w_in[layer], preferred_element_type=F32) + qkv_bias
        ).astype(BF)
        attended, log_totals = attend_forward(qkv, slots)
        attended, (piece,) = run_beside(
            normed_all, attended, cotangent_task(1 if layer == 0 else 2)
        )
        pieces[1 if layer == 0 else 2] = piece
        middle = stream + (
            scatter_rows(attended, times(w_out[layer]))[0]
            + outward_bias[layer]
        )
        normed_mid = layer_norm(middle, norm_gain[layer, 1], norm_shift[layer, 1]).astype(BF)
        mid_mine, _ = gather_ring(normed_mid)
        if layer == 0:
            mid_mine, w_down[0] = lax.optimization_barrier((mid_mine, w_down[0]))
        mid_all = gather_pair(mid_mine)
        hidden_pre = (
            jnp.dot(mid_all, w_up[layer], preferred_element_type=F32) + bias_up[layer]
        )
        activated = gelu_tanh(hidden_pre).astype(BF)
        saved.append(
            (stream, normed_all, qkv, attended, log_totals, middle, mid_all, hidden_pre,
             activated)
        )
        if layer == 0:
            activated, (pieces[-1],) = run_beside(mid_mine, activated, cotangent_task(-1))
            stream = middle + (
                scatter_rows(activated, times(w_down[layer]))[0]
                + shrink_bias[layer]
            )
            stream, w_in[1], w_out[1] = lax.optimization_barrier((stream, w_in[1], w_out[1]))
    cotangent_ring = jnp.concatenate([cotangent, pieces[1], pieces[-1], pieces[2]])

    grad_stream = cotangent.astype(F32)
    gains, shifts, sums_out, sums_down, sums_in, sums_up = {}, {}, {}, {}, {}, {}
    grads_mlp, grads_attn = [None] * LAYERS, [None] * LAYERS

    _, normed_all, qkv, attended, log_totals, middle, mid_all, hidden_pre, activated = saved[1]
    sums_down[1] = jnp.sum(cotangent, 0, dtype=F32)
    dy_all = gather_pair(cotangent_ring)

    def mlp_back(layer, dy_all):
        hidden_pre = saved[layer][7]
        grad_act = against_rows(dy_all, w_down[layer])
        du = jax.vjp(gelu_tanh, hidden_pre)[1](grad_act)[0].astype(BF)
        return du

    def mlp_sum(layer, du, dy_all, tasks):
        _, _, _, _, _, middle, mid_all, hidden_pre, activated = saved[layer]
        sums_up[layer] = jnp.sum(du, 0, dtype=F32)

        def make(dy_all, activated, mid_all, du):
            return grad_blocks([(dy_all, activated), (mid_all, du)])

        dh, results = scatter_rows(
            du, times_rows(w_up[layer]), [(make, (dy_all, activated, mid_all, du))] + tasks
        )
        back_mid = jax.vjp(layer_norm, middle, norm_gain[layer, 1], norm_shift[layer, 1])[1]
        grad_part, gains[layer, 1], shifts[layer, 1] = back_mid(dh)
        return grad_part, results

    def attn_sum(layer, dqkv, dz_all, tasks):
        stream, normed_all, _, attended, _, _, _, _, _ = saved[layer]
        sums = jnp.sum(dqkv, 0, dtype=F32)
        sums_in[layer] = jnp.stack([sums[:columns], sums[2 * columns :]])

        def make(dz_all, attended, normed_all, dqkv):
            return grad_blocks([(dz_all, attended), (normed_all, dqkv)])

        da, results = scatter_rows(
            dqkv, times_rows(w_in[layer]), [(make, (dz_all, attended, normed_all, dqkv))] + tasks
        )
        back_in = jax.vjp(layer_norm, stream, norm_gain[layer, 0], norm_shift[layer, 0])[1]
        grad_first, gains[layer, 0], shifts[layer, 0] = back_in(da)
        return grad_first, results

    du = mlp_back(1, dy_all)
    grad_part, (mlp1,) = mlp_sum(1, du, dy_all, [])
    grad_middle = grad_stream + grad_part
    mlp1 = send_x(mlp1)
    dz = grad_middle.astype(BF)
    sums_out[1] = jnp.sum(dz, 0, dtype=F32)
    dz_mine, _ = gather_ring(dz)
    dz_mine, near1 = lax.optimization_barrier((dz_mine, mlp1[:3]))
    dz_all = gather_pair(dz_mine)
    do = against_rows(dz_all, w_out[1]).astype(BF)
    dqkv = attend_backward(qkv, do, log_totals, slots)

    def last_pairs(activated):
        both = scatter_pair(activated, times(w_down[1]))
        low = both.astype(BF)
        rows = low.shape[0] // 4
        near = (
            both[:rows]
            + ring(low[rows : 2 * rows], "z", -1).astype(F32)
            + ring(low[2 * rows : 3 * rows], "z", 1).astype(F32)
        )
        return near, low[3 * rows :]

    dqkv, ((last_near, last_far),) = run_beside(dz_all, dqkv, [(last_pairs, (activated,))])
    dqkv, mlp1 = lax.optimization_barrier((dqkv, (*near1, mlp1[3])))
    mlp1 = send_y(*add_x(*mlp1))
    grad_first, (attn1, mlp1) = attn_sum(1, dqkv, dz_all, [(add_y, mlp1)])
    grad_stream = grad_middle + grad_first
    attn1 = send_x(attn1)
    grads_mlp[1] = send_core(*mlp1)

    _, normed_all, qkv, attended, log_totals, middle, mid_all, hidden_pre, activated = saved[0]
    dy = grad_stream.astype(BF)
    sums_down[0] = jnp.sum(dy, 0, dtype=F32)
    dy_mine, _ = gather_ring(dy)
    dy_mine, attn1 = lax.optimization_barrier((dy_mine, attn1))
    attn1 = send_y(*add_x(*attn1))
    dy_all = gather_pair(dy_mine)
    du = mlp_back(0, dy_all)
    du, (last_across,) = run_beside(
        dy_mine, du, [(lambda values: ring(values, "z", 2), (last_far,))]
    )
    hidden_out = saved[1][5] + (last_near + last_across.astype(F32) + shrink_bias[1])
    hidden_out = swap_halves(hidden_out.astype(BF)).astype(F32)
    du, attn1 = lax.optimization_barrier((du, attn1))
    grad_part, (mlp0, attn1) = mlp_sum(0, du, dy_all, [(add_y, attn1)])
    grad_middle = grad_stream + grad_part
    mlp0 = send_x(mlp0)
    grads_attn[1] = send_core(*attn1)
    dz = grad_middle.astype(BF)
    sums_out[0] = jnp.sum(dz, 0, dtype=F32)
    dz_mine, _ = gather_ring(dz)
    dz_mine, near0 = lax.optimization_barrier((dz_mine, mlp0[:3]))
    dz_all = gather_pair(dz_mine)
    do = against_rows(dz_all, w_out[0]).astype(BF)
    dqkv = attend_backward(qkv, do, log_totals, slots)
    dqkv, mlp0 = lax.optimization_barrier((dqkv, (*near0, mlp0[3])))
    mlp0 = send_y(*add_x(*mlp0))
    grad_first, (attn0, mlp0) = attn_sum(0, dqkv, dz_all, [(add_y, mlp0)])
    grad_stream = grad_middle + grad_first
    grad_hidden = swap_halves(grad_stream.astype(BF)).astype(F32)
    grads_mlp[0] = send_core(*mlp0)

    both = range(LAYERS)
    common = jnp.concatenate(
        [
            m.reshape(-1, 128)
            for m in (
                [gains[n, i] for n in both for i in (0, 1)]
                + [shifts[n, i] for n in both for i in (0, 1)]
                + [sums_out[n] for n in both]
                + [sums_down[n] for n in both]
            )
        ]
    )
    shard = jnp.concatenate(
        [m.reshape(-1, 128) for m in [sums_up[n] for n in both] + [sums_in[n] for n in both]]
    )
    common, shard, grads_attn[0] = sum_everywhere(
        common,
        shard,
        (
            lambda *m: m,
            lambda *m: send_y(*add_x(*m)),
            lambda *m: send_core(*add_y(*m)),
        ),
        send_x(attn0),
    )
    grad_gain = common[:32].reshape(LAYERS, 2, 1024)
    grad_shift = common[32:64].reshape(LAYERS, 2, 1024)
    grad_out_bias = common[64:80].reshape(LAYERS, 1024)
    grad_down_bias = common[80:96].reshape(LAYERS, 1024)
    grad_up_bias = shard[:8].reshape(LAYERS, -1)
    grad_in_bias = shard[8:].reshape(LAYERS, 2, columns)

    width = shrink.shape[1]
    return (
        hidden_out,
        grad_hidden,
        grad_gain,
        grad_shift,
        jnp.stack([g[:, columns:].reshape(-1, 3, columns) for g in grads_attn]),
        grad_in_bias,
        jnp.stack([g[:, :columns].T for g in grads_attn]),
        grad_out_bias,
        jnp.stack([g[:, width:] for g in grads_mlp]),
        grad_up_bias,
        jnp.stack([g[:, :width].T for g in grads_mlp]),
        grad_down_bias,
    )


def solution(mesh):
    fine = Mesh(mesh.devices.reshape(2, 4, 2, 2, 4), ("yh", "x", "c", "yl", "z"))
    dp, tensor = ("yh", "x", "c"), ("yl", "z")
    rows = P(dp + tensor, None)
    return jax.shard_map(
        per_device,
        mesh=fine,
        in_specs=(
            rows,
            rows,
            P(),
            P(),
            P(None, None, None, tensor),
            P(None, None, tensor),
            P(None, tensor, None),
            P(),
            P(None, None, tensor),
            P(None, tensor),
            P(None, tensor, None),
            P(),
        ),
        out_specs=(
            rows,
            rows,
            P(),
            P(),
            P(None, dp, None, tensor),
            P(None, None, tensor),
            P(None, tensor, dp),
            P(),
            P(None, dp, tensor),
            P(None, tensor),
            P(None, tensor, dp),
            P(),
        ),
        check_vma=False,
    )
```
